256 devices in a mesh: ent: 64 (over x, z, core), rel: 4 (over y).
Axes of the slice: x: 4, y: 4, z: 8, core: 2. Of those that a mesh axis runs over, the one named last changes fastest.
Arguments:
- feats: bfloat16 [32768, 512], P('ent'), may hold values from -6 to 6
- cotangent: bfloat16 [32768, 512], P('ent'), may hold values from -6 to 6
- bases: bfloat16 [8, 512, 512], P('rel'), may hold values from -0.25 to 0.25
- coeffs: float32 [824, 8], P('rel'), may hold values from -3 to 3
- send_rows: int32 [4096, 16], P('ent'), may hold values from 0 to 511
- tile_rel: int32 [64, 128], P('ent', 'rel'), may hold values from 0 to 205
- tile_row: int32 [64, 128], P('ent', 'rel'), may hold values from 0 to 3
- tile_col: int32 [64, 128], P('ent', 'rel'), may hold values from 0 to 11
- tile_edges: int32 [64, 128, 256], P('ent', 'rel'), may hold values from 0 to 16383
- tile_live: int32 [64, 4], P('ent', 'rel'), may hold values from 8 to 32, as said below
Outputs:
- entity_grads: float32 [32768, 512], P('ent', 'rel')
- basis_grads: float32 [8, 512, 512], P('rel', 'ent')
- coeff_grads: float32 [824, 8], P('rel')
The draws below stay inside these ranges and needn't reach their ends.
Inputs may be any that keep to these rules, and one draw needn't show every extreme that they name: `tile_live`: some device holds exactly 32 used slots in every draw; every device holds at least a quarter of that. `tile_edges`: repeated entries are parallel edges.
All inputs are finite; a program needn't handle non-finite values.
Results may differ from the reference program's by a relative error of at most 0.015.
Values may be sent and summed in bfloat16 or wider, within the bound.
A program may use at most 128 MiB of HBM per device.

```python
import jax
import jax.numpy as jnp
from jax import lax

D = 512
BASES = 8
REL_DEV = 206
TILE = 128
EDGE_TILE = 256
ENT_DEV = 512
HALO_PEER = 16
TILE_DEV = 32
RELATIONS = 824
ENTITIES = 32768
COL_BLOCKS = 12
N_ENT = 64
N_REL = 4


def draw_tile_live(key, part):
    key = jax.random.fold_in(key, 7)
    first, second = jax.random.split(key)
    shifts = jax.random.randint(first, (N_ENT * N_REL,), 0, 3).astype(jnp.int32)
    counts = jnp.right_shift(jnp.full((N_ENT * N_REL,), TILE_DEV, jnp.int32), shifts)
    chosen = jax.random.randint(second, (), 0, N_ENT * N_REL).astype(jnp.int32)
    counts = counts.at[chosen].set(TILE_DEV)
    return counts.reshape(N_ENT, N_REL)


def set_ends(drawn, stream_key, least, high):
    extent = drawn.shape
    index_at = [jax.random.randint(jax.random.fold_in(stream_key, axis), (), 0, extent[axis]) for axis in range(len(extent))]
    drawn = drawn.at[tuple(index_at)].set(least)
    longest = extent.index(max(extent))
    index_at[longest] = (index_at[longest] + 1) % extent[longest]
    return drawn.at[tuple(index_at)].set(high)


def levels(stream_key, dims, cuts, low, top_value):
    def one(position, shards_of):
        draws = jax.random.uniform(jax.random.fold_in(jax.random.fold_in(stream_key, 6), position), (shards_of,), jnp.float32, low / len(cuts), top_value / len(cuts))
        return jnp.repeat(jnp.exp(draws), dims[position] // shards_of).reshape((-1,) + (1,) * (len(dims) - position - 1))

    loudness = one(*cuts[0])
    for cut in cuts[1:]:
        loudness = loudness * one(*cut)
    return loudness


def centred(own_key, dims, width, reach, cuts=(), held_as=jnp.bfloat16):
    gain = levels(own_key, dims, cuts, -0.22, 0.18) if cuts else 1.0
    entries = jax.random.normal(own_key, dims, jnp.float32) * width * gain
    return jnp.minimum(jnp.maximum(entries, -reach), reach).astype(held_as)


def setup_inputs(seed: int = 0) -> dict:
    splits = jax.random.split(jax.random.key(seed), 11)
    return {
        "feats": centred(splits[0], (ENTITIES, D), 1.0, 6.0, ((0, 64),)),
        "cotangent": centred(splits[1], (ENTITIES, D), 1.0, 6.0, ((0, 64),)),
        "bases": centred(splits[2], (BASES, D, D), D ** -0.5, 0.25, ((0, 4),)),
        "coeffs": centred(splits[3], (RELATIONS, BASES), 0.5, 3.0, ((0, 4),), jnp.float32),
        "send_rows": set_ends(jax.random.randint(splits[4], (N_ENT * N_ENT, HALO_PEER), 0, ENT_DEV), jax.random.fold_in(splits[4], 1), 0, ENT_DEV - 1).astype(jnp.int32),
        "tile_rel": set_ends(jax.random.randint(splits[5], (N_ENT, N_REL * TILE_DEV), 0, REL_DEV), jax.random.fold_in(splits[5], 1), 0, REL_DEV - 1).astype(jnp.int32),
        "tile_row": set_ends(jax.random.randint(splits[6], (N_ENT, N_REL * TILE_DEV), 0, ENT_DEV // TILE), jax.random.fold_in(splits[6], 1), 0, (ENT_DEV // TILE) - 1).astype(jnp.int32),
        "tile_col": set_ends(jax.random.randint(splits[7], (N_ENT, N_REL * TILE_DEV), 0, COL_BLOCKS), jax.random.fold_in(splits[7], 1), 0, COL_BLOCKS - 1).astype(jnp.int32),
        "tile_edges": set_ends(jax.random.randint(splits[8], (N_ENT, N_REL * TILE_DEV, EDGE_TILE), 0, TILE * TILE), jax.random.fold_in(splits[8], 1), 0, (TILE * TILE) - 1).astype(jnp.int32),
        "tile_live": draw_tile_live(jax.random.fold_in(splits[10], 71), 0),
    }


HIGH = lax.Precision.HIGHEST


def inverse_degree(rel_ids, row_ids, edge_ids, live, rel_count, row_blocks):
    count = edge_ids.shape[0]
    places = jnp.arange(TILE, dtype=jnp.int32)
    alive = (jnp.arange(count, dtype=jnp.int32) < live).astype(jnp.float32)
    row_sums = jnp.sum(((edge_ids // TILE)[:, :, None] == places).astype(jnp.float32), axis=1) * alive[:, None]
    rel_hot = (rel_ids[:, None] == jnp.arange(rel_count, dtype=jnp.int32)).astype(jnp.float32)
    row_hot = (row_ids[:, None] == jnp.arange(row_blocks, dtype=jnp.int32)).astype(jnp.float32)
    degree = jnp.einsum("tr,tk,ti->rki", rel_hot, row_hot, row_sums, precision=HIGH)
    return 1.0 / jnp.maximum(degree, 1.0)


def tile_terms(extended, dm_blocks, coeff_group, inverse, rel_ids, row_ids, col_ids, edge_ids, alive):
    rel_count = coeff_group.shape[0]
    row_blocks = dm_blocks.shape[0]
    col_blocks = extended.shape[0] // TILE
    places = jnp.arange(TILE, dtype=jnp.int32)
    row_edges = ((edge_ids // TILE)[:, :, None] == places).astype(jnp.float32)
    col_edges = ((edge_ids % TILE)[:, :, None] == places).astype(jnp.float32)
    adjacency = jnp.einsum("tei,tej->tij", row_edges, col_edges) * alive[:, None, None]
    rel_hot = (rel_ids[:, None] == jnp.arange(rel_count, dtype=jnp.int32)).astype(jnp.float32)
    row_hot = (row_ids[:, None] == jnp.arange(row_blocks, dtype=jnp.int32)).astype(jnp.float32)
    col_hot = (col_ids[:, None] == jnp.arange(col_blocks, dtype=jnp.int32)).astype(jnp.float32)
    inv_tile = jnp.einsum("tr,tk,rki->ti", rel_hot, row_hot, inverse, precision=HIGH)
    columns = jnp.take(extended.reshape(col_blocks, TILE, -1), col_ids, axis=0).astype(jnp.float32)
    products = jnp.einsum("tij,tjd->tid", adjacency, columns, precision=HIGH)
    scaled = inv_tile[:, :, None] * products
    coeff_tile = jnp.dot(rel_hot, coeff_group, precision=HIGH)
    weight = row_hot[:, :, None] * coeff_tile[:, None, :]
    dm_wide = dm_blocks.astype(jnp.float32)
    partial_value = jnp.einsum("tkb,tid->kbid", weight, scaled, precision=HIGH)
    inner = jnp.einsum("tid,kbid->tkb", scaled, dm_wide, precision=HIGH)
    coeff_part = jnp.einsum("tr,tk,tkb->rb", rel_hot, row_hot, inner, precision=HIGH)
    pulled = inv_tile[:, :, None] * jnp.einsum("tkb,kbid->tid", weight, dm_wide, precision=HIGH)
    pulled = pulled.astype(jnp.bfloat16).astype(jnp.float32)
    back = jnp.einsum("tij,tid->tjd", adjacency, pulled, precision=HIGH)
    ext_part = jnp.einsum("tc,tjd->cjd", col_hot, back, precision=HIGH).reshape(col_blocks * TILE, -1)
    return partial_value, coeff_part, ext_part


def reference(feats, cotangent, bases, coeffs, send_rows, tile_rel, tile_row, tile_col, tile_edges, tile_live):
    row_blocks = ENT_DEV // TILE
    sends = send_rows.reshape(N_ENT, N_ENT, HALO_PEER)
    owners = jnp.arange(N_ENT, dtype=jnp.int32)[:, None] * ENT_DEV
    bases_wide = bases.astype(jnp.float32)
    slot_ids = jnp.arange(TILE_DEV, dtype=jnp.int32)

    def device_step(carry, device):
        grads, basis_total, coeff_total = carry
        own_rows = device * ENT_DEV + jnp.arange(ENT_DEV, dtype=jnp.int32)
        halo_rows = (lax.dynamic_index_in_dim(sends, device, 1, keepdims=False) + owners).reshape(-1)
        extended = jnp.concatenate([feats[own_rows], feats[halo_rows]], axis=0)
        cot_blocks = cotangent[own_rows].reshape(row_blocks, TILE, D).astype(jnp.float32)
        dm_blocks = jnp.einsum("kro,bio->kbri", cot_blocks, bases_wide, precision=HIGH).astype(jnp.bfloat16)
        totals = jnp.zeros((row_blocks, BASES, TILE, D), jnp.float32)
        ext_total = jnp.zeros((ENT_DEV + N_ENT * HALO_PEER, D), jnp.float32)
        rel_row = lax.dynamic_index_in_dim(tile_rel, device, 0, keepdims=False)
        row_row = lax.dynamic_index_in_dim(tile_row, device, 0, keepdims=False)
        col_row = lax.dynamic_index_in_dim(tile_col, device, 0, keepdims=False)
        edge_row = lax.dynamic_index_in_dim(tile_edges, device, 0, keepdims=False)
        live_row = lax.dynamic_index_in_dim(tile_live, device, 0, keepdims=False)
        for group in range(N_REL):
            lo = group * TILE_DEV
            hi = lo + TILE_DEV
            live = live_row[group]
            rel_ids = rel_row[lo:hi]
            row_ids = row_row[lo:hi]
            edge_ids = edge_row[lo:hi]
            coeff_group = coeffs[group * REL_DEV:(group + 1) * REL_DEV]
            inverse = inverse_degree(rel_ids, row_ids, edge_ids, live, REL_DEV, row_blocks)
            alive = (slot_ids < live).astype(jnp.float32)
            partial_value, coeff_part, ext_part = tile_terms(extended, dm_blocks, coeff_group, inverse, rel_ids, row_ids, col_row[lo:hi], edge_ids, alive)
            rounded = lax.optimization_barrier(partial_value.astype(jnp.bfloat16))
            totals = totals + rounded.astype(jnp.float32)
            coeff_total = coeff_total.at[group * REL_DEV:(group + 1) * REL_DEV].add(coeff_part)
            ext_total = ext_total + ext_part
        mixed = lax.optimization_barrier(totals.astype(jnp.bfloat16)).astype(jnp.float32)
        basis_total = basis_total + jnp.einsum("kbri,kro->bio", mixed, cot_blocks, precision=HIGH)
        grads = grads.at[own_rows].add(ext_total[:ENT_DEV]).at[halo_rows].add(ext_total[ENT_DEV:])
        return (grads, basis_total, coeff_total), None

    start = (jnp.zeros((ENTITIES, D), jnp.float32), jnp.zeros((BASES, D, D), jnp.float32), jnp.zeros((RELATIONS, BASES), jnp.float32))
    (grads, basis_total, coeff_total), _ = lax.scan(device_step, start, jnp.arange(N_ENT, dtype=jnp.int32))
    return grads, basis_total, coeff_total
```

```python
import functools

import jax
import jax.numpy as jnp
from jax import lax
from jax.experimental import pallas as pl
from jax.experimental.pallas import tpu as pltpu
from jax.sharding import PartitionSpec as P

TILE = 128
LANES = 128
BF16 = jnp.bfloat16
F32 = jnp.float32
HIGH = lax.Precision.HIGHEST
VMEM = pl.BlockSpec(memory_space=pltpu.VMEM)
SMEM = pl.BlockSpec(memory_space=pltpu.SMEM)


def tiles_kernel(edges_ref, meta_ref, adj_ref, inv_ref, sums_ref):
    slots, listed = edges_ref.shape
    place = lax.broadcasted_iota(jnp.int32, (TILE, listed), 0).astype(BF16)

    def build(t, carry):
        edge = edges_ref[pl.ds(t, 1), :]
        col = (edge & (TILE - 1)).astype(BF16)
        row = (edge >> 7).astype(BF16)
        one, zero = jnp.ones((), BF16), jnp.zeros((), BF16)
        col_hot = jnp.where(place == col, one, zero)
        row_hot = jnp.where(place == row, one, zero)
        counts = lax.dot_general(
            col_hot, row_hot, (((1,), (1,)), ((), ())), preferred_element_type=F32
        )
        adj_ref[t] = counts.astype(BF16)
        sums_ref[pl.ds(t, 1), :] = jnp.sum(counts, axis=0, keepdims=True)
        return carry

    lax.fori_loop(0, slots, build, 0, unroll=4)
    key = jnp.broadcast_to(meta_ref[0:1, :], (slots, slots))
    live = jnp.broadcast_to(meta_ref[1:2, :], (slots, slots))
    same = jnp.where(key == key.T, live, 0.0).astype(BF16)
    degree = jnp.dot(same, sums_ref[...].astype(BF16), preferred_element_type=F32)
    inv_ref[...] = live.T / jnp.maximum(degree, 1.0)


def main_kernel(
    spots_ref,
    coef_ref,
    adj_ref,
    inv_ref,
    ext_ref,
    ext_t_ref,
    cot_ref,
    bases_ref,
    basis_ref,
    grads_ref,
    inner_ref,
    wide_ref,
    dm_ref,
    *,
    groups,
):
    bases_count, rows, width = wide_ref.shape
    slots = adj_ref.shape[0]
    per_group = slots // groups

    def scaled(t):
        return adj_ref[t].astype(F32) * inv_ref[pl.ds(t, 1), :]

    def block(t):
        row = pl.multiple_of(spots_ref[0, t] * TILE, TILE)
        col = pl.multiple_of(spots_ref[1, t] * TILE, TILE)
        return pl.ds(col, TILE), pl.ds(row, TILE)

    def clear(c, carry):
        for b in range(bases_count):
            wide_ref[b, pl.ds(pl.multiple_of(c * TILE, TILE), TILE), :] = jnp.zeros(
                (TILE, width), F32
            )
        return carry

    lax.fori_loop(0, rows // TILE, clear, 0)

    def place(t, carry):
        value = scaled(t)
        at = block(t)
        for b in range(bases_count):
            wide_ref[(b, *at)] += coef_ref[b, t] * value
        return carry

    for g in range(groups):
        lax.fori_loop(g * per_group, g * per_group + spots_ref[2, g], place, 0)

    grads_ref[...] = jnp.zeros_like(grads_ref)

    def both(b, carry):
        dm = lax.dot_general(
            bases_ref[b], cot_ref[...], (((1,), (1,)), ((), ())), preferred_element_type=F32
        ).astype(BF16)
        dm_ref[b] = dm
        weights = wide_ref[b].astype(BF16)
        grads_ref[...] += lax.dot_general(
            weights, dm, (((1,), (1,)), ((), ())), preferred_element_type=F32
        )
        mixed = jnp.dot(ext_t_ref[...], weights, preferred_element_type=F32).astype(BF16)
        basis_ref[b] = jnp.dot(mixed, cot_ref[...], preferred_element_type=F32)
        return carry

    lax.fori_loop(0, bases_count, both, 0)

    def spread(b, carry):
        wide_ref[b] = jnp.dot(ext_ref[...], dm_ref[b], preferred_element_type=F32)
        return carry

    lax.fori_loop(0, bases_count, spread, 0)
    inner_ref[...] = jnp.zeros_like(inner_ref)

    def measure(t, carry):
        value = scaled(t)
        at = block(t)
        for b in range(bases_count):
            inner_ref[b, pl.ds(t, 1), :] = jnp.sum(
                value * wide_ref[(b, *at)], axis=0, keepdims=True
            )
        return carry

    for g in range(groups):
        lax.fori_loop(g * per_group, g * per_group + spots_ref[2, g], measure, 0)


def per_device(
    feats, cotangent, bases, coeffs, send_rows, tile_rel, tile_row, tile_col, tile_edges, tile_live
):
    ent_rows, width = feats.shape
    groups = lax.axis_size("rel")
    ents = lax.axis_size("ent")
    g = lax.axis_index("rel")
    share = width // groups
    rel_count, bases_count = coeffs.shape
    slots = tile_rel.shape[1]
    all_slots = slots * groups
    own_bases = bases.shape[0]

    rel_hot = tile_rel[0][:, None] == jnp.arange(rel_count, dtype=jnp.int32)
    coef = jnp.dot(rel_hot.astype(F32), coeffs, precision=HIGH)
    alive = jnp.arange(slots, dtype=jnp.int32) < tile_live[0, 0]
    key = (g * rel_count + tile_rel[0]) * 4 + tile_row[0]
    lists = jnp.concatenate(
        [
            tile_edges[0].astype(F32),
            coef,
            key[:, None].astype(F32),
            alive[:, None].astype(F32),
            tile_row[0][:, None].astype(F32),
            tile_col[0][:, None].astype(F32),
        ],
        axis=1,
    )
    lists = lax.all_gather(lists, "rel", axis=0, tiled=True)
    listed = tile_edges.shape[2]
    edges = lists[:, :listed].astype(jnp.int32)
    meta = lists[:, listed:].T
    coef_all = meta[:bases_count]
    marks = meta[bases_count : bases_count + 2]
    spots = meta[bases_count + 2 :].astype(jnp.int32)
    lives = jnp.sum(marks[1].reshape(groups, slots), axis=1).astype(jnp.int32)
    spots = jnp.concatenate([spots, jnp.pad(lives, (0, all_slots - groups))[None]], axis=0)

    own = lax.dynamic_slice_in_dim(feats, g * share, share, 1)
    flat_rows = send_rows.reshape(-1)
    pick = (flat_rows[:, None] == jnp.arange(ent_rows, dtype=jnp.int32)).astype(BF16)
    outgoing = jnp.dot(pick, own, preferred_element_type=F32).astype(BF16)
    incoming = lax.all_to_all(outgoing, "ent", split_axis=0, concat_axis=0, tiled=True)
    extended = jnp.concatenate([own, incoming], axis=0)
    all_bases = lax.all_to_all(bases, "rel", split_axis=1, concat_axis=0, tiled=True)

    adj, inv = pl.pallas_call(
        tiles_kernel,
        out_shape=(
            jax.ShapeDtypeStruct((all_slots, TILE, TILE), BF16),
            jax.ShapeDtypeStruct((all_slots, TILE), F32),
        ),
        in_specs=[VMEM] * 2,
        out_specs=(VMEM, VMEM),
        scratch_shapes=[pltpu.VMEM((all_slots, TILE), F32)],
        compiler_params=pltpu.CompilerParams(vmem_limit_bytes=32 << 20),
    )(edges, marks)

    rows = extended.shape[0]
    basis, grads, inner = pl.pallas_call(
        functools.partial(main_kernel, groups=groups),
        out_shape=(
            jax.ShapeDtypeStruct((bases_count, share, width), F32),
            jax.ShapeDtypeStruct((rows, share), F32),
            jax.ShapeDtypeStruct((bases_count, all_slots, TILE), F32),
        ),
        in_specs=[SMEM, SMEM] + [VMEM] * 6,
        out_specs=(VMEM,) * 3,
        scratch_shapes=[
            pltpu.VMEM((bases_count, rows, ent_rows), F32),
            pltpu.VMEM((bases_count, share, ent_rows), BF16),
        ],
        compiler_params=pltpu.CompilerParams(vmem_limit_bytes=56 << 20),
    )(spots, coef_all, adj, inv, extended, extended.T, cotangent, all_bases)

    halo = grads[ent_rows:].astype(BF16)
    returned = lax.all_to_all(halo, "ent", split_axis=0, concat_axis=0, tiled=True)
    entity_grads = grads[:ent_rows] + jnp.dot(pick.T, returned, preferred_element_type=F32)

    cores, zs = 2, ents // (2 * groups)
    part = basis.reshape(groups, own_bases, zs, cores, -1, width)
    part = jnp.transpose(part, (0, 2, 3, 1, 4, 5)).reshape(ents, -1, width)
    part = lax.psum_scatter(part, "ent", scatter_dimension=0, tiled=True)[0]
    swap = []
    for x in range(groups):
        for rest in range(ents // groups):
            for y in range(groups):
                swap.append(
                    ((x * (ents // groups) + rest) * groups + y, (y * (ents // groups) + rest) * groups + x)
                )
    basis_grads = lax.ppermute(part, ("ent", "rel"), swap).reshape(own_bases, -1, width)

    tile_part = jnp.sum(inner, axis=2).T
    tile_part = lax.psum_scatter(tile_part, "rel", scatter_dimension=0, tiled=True)
    coeff_part = jnp.dot(rel_hot.astype(F32).T, tile_part, precision=HIGH)
    coeff_grads = lax.psum(coeff_part, "ent")
    return entity_grads, basis_grads, coeff_grads


def solution(mesh):
    placed = (
        P("ent", None),
        P("ent", None),
        P("rel", None, None),
        P("rel", None),
        P("ent", None),
        P("ent", "rel"),
        P("ent", "rel"),
        P("ent", "rel"),
        P("ent", "rel", None),
        P("ent", "rel"),
    )
    return jax.shard_map(
        per_device,
        mesh=mesh,
        in_specs=placed,
        out_specs=(P("ent", "rel"), P("rel", "ent", None), P("rel", None)),
        check_vma=False,
    )
```

```python
import functools

import jax
import jax.numpy as jnp
from jax import lax
from jax.experimental import pallas as pl
from jax.experimental.pallas import tpu as pltpu
from jax.sharding import PartitionSpec as P

TILE = 128
LANES = 128
BF16 = jnp.bfloat16
F32 = jnp.float32
HIGH = lax.Precision.HIGHEST
VMEM = pl.BlockSpec(memory_space=pltpu.VMEM)
SMEM = pl.BlockSpec(memory_space=pltpu.SMEM)


def tiles_kernel(edges_ref, meta_ref, adj_ref, inv_ref, sums_ref):
    slots, listed = edges_ref.shape
    place = lax.broadcasted_iota(jnp.int32, (TILE, listed), 0).astype(BF16)

    def build(t, carry):
        edge = edges_ref[pl.ds(t, 1), :]
        col = (edge & (TILE - 1)).astype(BF16)
        row = (edge >> 7).astype(BF16)
        one, zero = jnp.ones((), BF16), jnp.zeros((), BF16)
        col_hot = jnp.where(place == col, one, zero)
        row_hot = jnp.where(place == row, one, zero)
        counts = lax.dot_general(
            col_hot, row_hot, (((1,), (1,)), ((), ())), preferred_element_type=F32
        )
        adj_ref[t] = counts.astype(BF16)
        sums_ref[pl.ds(t, 1), :] = jnp.sum(counts, axis=0, keepdims=True)
        return carry

    lax.fori_loop(0, slots, build, 0, unroll=4)
    key = jnp.broadcast_to(meta_ref[0:1, :], (slots, slots))
    live = jnp.broadcast_to(meta_ref[1:2, :], (slots, slots))
    same = jnp.where(key == key.T, live, 0.0).astype(BF16)
    degree = jnp.dot(same, sums_ref[...].astype(BF16), preferred_element_type=F32)
    inv_ref[...] = live.T / jnp.maximum(degree, 1.0)


def main_kernel(
    spots_ref,
    coef_ref,
    adj_ref,
    inv_ref,
    ext_ref,
    ext_t_ref,
    cot_ref,
    bases_ref,
    basis_ref,
    own_ref,
    halo_ref,
    parts_ref,
    wide_ref,
    dm_ref,
    grads_ref,
    inner_ref,
    *,
    groups,
):
    bases_count, rows, width = wide_ref.shape
    cores, pairs, zs, lines, _ = basis_ref.shape
    each = bases_count // pairs
    strip = lines // each
    slots = adj_ref.shape[0]
    per_group = slots // groups

    def scaled(t):
        return adj_ref[t].astype(F32) * inv_ref[pl.ds(t, 1), :]

    def block(t):
        row = pl.multiple_of(spots_ref[0, t] * TILE, TILE)
        col = pl.multiple_of(spots_ref[1, t] * TILE, TILE)
        return pl.ds(col, TILE), pl.ds(row, TILE)

    def clear(c, carry):
        for b in range(bases_count):
            wide_ref[b, pl.ds(pl.multiple_of(c * TILE, TILE), TILE), :] = jnp.zeros(
                (TILE, width), F32
            )
        return carry

    lax.fori_loop(0, rows // TILE, clear, 0)

    def place(t, carry):
        value = scaled(t)
        at = block(t)
        for b in range(bases_count):
            wide_ref[(b, *at)] += coef_ref[b, t] * value
        return carry

    for g in range(groups):
        lax.fori_loop(g * per_group, g * per_group + spots_ref[2, g], place, 0)

    grads_ref[...] = jnp.zeros_like(grads_ref)

    def both(pair, carry):
        results = []
        for one in range(each):
            b = pair * each + one
            dm = lax.dot_general(
                bases_ref[b], cot_ref[...], (((1,), (1,)), ((), ())), preferred_element_type=F32
            ).astype(BF16)
            dm_ref[b] = dm
            weights = wide_ref[b].astype(BF16)
            grads_ref[...] += lax.dot_general(
                weights, dm, (((1,), (1,)), ((), ())), preferred_element_type=F32
            )
            mixed = jnp.dot(ext_t_ref[...], weights, preferred_element_type=F32).astype(BF16)
            results.append(jnp.dot(mixed, cot_ref[...], preferred_element_type=F32))
        for z in range(zs):
            for core in range(cores):
                at = (z * cores + core) * strip
                basis_ref[core, pair, z] = jnp.concatenate(
                    [r[at : at + strip] for r in results], axis=0
                ).astype(BF16)
        return carry

    lax.fori_loop(0, pairs, both, 0)
    own_ref[...] = grads_ref[: own_ref.shape[0], :]
    halo_ref[...] = grads_ref[own_ref.shape[0] :, :].astype(BF16)

    def spread(b, carry):
        wide_ref[b] = jnp.dot(ext_ref[...], dm_ref[b], preferred_element_type=F32)
        return carry

    lax.fori_loop(0, bases_count, spread, 0)
    inner_ref[...] = jnp.zeros_like(inner_ref)

    def measure(t, carry):
        value = scaled(t)
        at = block(t)
        for b in range(bases_count):
            inner_ref[b, pl.ds(t, 1), :] = jnp.sum(
                value * wide_ref[(b, *at)], axis=0, keepdims=True
            )
        return carry

    for g in range(groups):
        lax.fori_loop(g * per_group, g * per_group + spots_ref[2, g], measure, 0)
    for b in range(bases_count):
        parts_ref[pl.ds(b, 1), :] = jnp.sum(inner_ref[b].T, axis=0, keepdims=True)


def share_kernel(
    basis_ref,
    own_ref,
    halo_ref,
    rows_ref,
    parts_ref,
    key_ref,
    grads_out,
    basis_out,
    coeff_out,
    back_ref,
    core_in,
    x_out,
    x_in,
    x_sum,
    z_out,
    z_in,
    final_ref,
    c_rel,
    c_core,
    c_x,
    c_z,
    halo_sems,
    core_sems,
    x_sems,
    z_sems,
    swap_sems,
    c_rel_sems,
    c_core_sems,
    c_x_sems,
    c_z_sems,
):
    cores, xs, zs, lines, width = basis_ref.shape
    ents = cores * xs * zs
    peer_rows = halo_ref.shape[0] // ents
    groups = xs
    d, y = lax.axis_index("ent"), lax.axis_index("rel")
    core = lax.rem(d, cores)
    z = lax.rem(lax.div(d, cores), zs)
    x = lax.div(d, cores * zs)

    def ent(x_at, z_at, core_at):
        return (x_at * zs + z_at) * cores + core_at

    def send(src, dst, sems, at, to_ent, to_rel):
        return pltpu.make_async_remote_copy(
            src_ref=src,
            dst_ref=dst,
            send_sem=sems.at[0, at],
            recv_sem=sems.at[1, at],
            device_id=(to_ent, to_rel),
            device_id_type=pl.DeviceIdType.MESH,
        )

    barrier = pltpu.get_barrier_semaphore()

    def greet(to_ent, to_rel):
        pl.semaphore_signal(
            barrier, inc=1, device_id=(to_ent, to_rel), device_id_type=pl.DeviceIdType.MESH
        )

    def greet_ent(off, carry):
        greet(lax.rem(d + off, ents), y)
        return carry

    lax.fori_loop(1, ents, greet_ent, 0)
    for k in range(1, groups):
        greet(d, lax.rem(y + k, groups))
    other = ent(y, z, core)

    @pl.when(x != y)
    def _():
        greet(other, x)

    pl.semaphore_wait(barrier, ents - 1 + groups - 1 + jnp.where(x != y, 1, 0))

    c_rel_copies = [
        send(parts_ref, c_rel.at[k], c_rel_sems, k, d, lax.rem(y + k, groups))
        for k in range(1, groups)
    ]
    for copy in c_rel_copies:
        copy.start()
    order = (2, 1, 3, 0)
    mate = d + 1 - 2 * core
    core_copies = {}
    for k in order:
        to_x = lax.rem(x + k, xs)
        core_copies[k] = send(
            basis_ref.at[1 - core, to_x], core_in.at[k], core_sems, k, mate, y
        )
        core_copies[k].start()

    def halo_copy(off):
        to = lax.rem(d + off, ents)
        return send(
            halo_ref.at[pl.ds(pl.multiple_of(to * peer_rows, peer_rows), peer_rows), :],
            back_ref.at[pl.ds(pl.multiple_of(d * peer_rows, peer_rows), peer_rows), :],
            halo_sems,
            off,
            to,
            y,
        )

    def halo_start(off, carry):
        halo_copy(off).start()
        return carry

    lax.fori_loop(1, ents, halo_start, 0)
    mine = pl.ds(pl.multiple_of(d * peer_rows, peer_rows), peer_rows)
    back_ref[mine, :] = halo_ref[mine, :]

    total = parts_ref[...]
    for k in range(1, groups):
        c_rel_copies[k - 1].wait()
        total = total + c_rel[k]
    rel_count = coeff_out.shape[0]
    slots = key_ref.shape[1]
    padded = c_core.shape[2]
    relation = lax.broadcasted_iota(jnp.int32, (padded, slots), 0) + y * rel_count
    hot = jnp.where(relation == key_ref[...], 1.0, 0.0)
    by_relation = lax.dot_general(
        total, hot, (((1,), (1,)), ((), ())), preferred_element_type=F32, precision=HIGH
    )
    c_core[0] = by_relation
    c_core_copy = send(c_core.at[0], c_core.at[1], c_core_sems, 0, mate, y)
    c_core_copy.start()

    x_copies = {}
    for k in order:
        core_copies[k].wait()
        to_x = lax.rem(x + k, xs)
        value = basis_ref[core, to_x].astype(F32) + core_in[k].astype(F32)
        if k == 0:
            x_sum[...] = value
        else:
            x_out[k] = value.astype(BF16)
            x_copies[k] = send(
                x_out.at[k], x_in.at[k], x_sems, k, ent(to_x, z, core), y
            )
            x_copies[k].start()

    c_core_copy.wait()
    c_x[x] = c_core[0] + c_core[1]
    c_x_copies = [
        send(c_x.at[x], c_x.at[x], c_x_sems, k, ent(lax.rem(x + k, xs), z, core), y)
        for k in range(1, xs)
    ]
    for copy in c_x_copies:
        copy.start()

    for k in range(1, xs):
        x_copies[k].wait()
    z_copies = []
    for k in range(1, zs):
        to_z = lax.rem(z + k, zs)
        value = x_sum[to_z]
        for j in range(1, xs):
            value = value + x_in[j, to_z].astype(F32)
        z_out[k] = value.astype(BF16)
        copy = send(z_out.at[k], z_in.at[k], z_sems, k, ent(x, to_z, core), y)
        copy.start()
        z_copies.append(copy)
    value = x_sum[z]
    for j in range(1, xs):
        value = value + x_in[j, z].astype(F32)

    for copy in c_x_copies:
        copy.wait()
    total = c_x[0]
    for j in range(1, xs):
        total = total + c_x[j]
    c_z[z] = total
    c_z_copies = [
        send(c_z.at[z], c_z.at[z], c_z_sems, k, ent(x, lax.rem(z + k, zs), core), y)
        for k in range(1, zs)
    ]
    for copy in c_z_copies:
        copy.start()

    for k in range(1, zs):
        z_copies[k - 1].wait()
        value = value + z_in[k].astype(F32)
    final_ref[...] = value.reshape(final_ref.shape)
    swap = send(final_ref, basis_out, swap_sems, 0, other, x)

    @pl.when(x != y)
    def _():
        swap.start()

    def halo_wait(off, carry):
        halo_copy(off).wait()
        return carry

    lax.fori_loop(1, ents, halo_wait, 0)
    ent_rows = own_ref.shape[0]
    returned = back_ref.shape[0]
    step = 256
    for at in range(0, returned, step):
        row = lax.broadcasted_iota(jnp.int32, (ent_rows, step), 0)
        hot = jnp.where(row == rows_ref[:, at : at + step], 1.0, 0.0).astype(BF16)
        more = jnp.dot(hot, back_ref[at : at + step, :], preferred_element_type=F32)
        base = own_ref[...] if at == 0 else grads_out[...]
        grads_out[...] = base + more

    for copy in c_z_copies:
        copy.wait()
    total = c_z[0]
    for j in range(1, zs):
        total = total + c_z[j]
    coeff_out[...] = total.T[:rel_count, :]

    @pl.when(x != y)
    def _():
        swap.wait()

    @pl.when(x == y)
    def _():
        basis_out[...] = final_ref[...]


def per_device(
    feats, cotangent, bases, coeffs, send_rows, tile_rel, tile_row, tile_col, tile_edges, tile_live
):
    ent_rows, width = feats.shape
    groups = lax.axis_size("rel")
    ents = lax.axis_size("ent")
    g = lax.axis_index("rel")
    share = width // groups
    rel_count, bases_count = coeffs.shape
    slots = tile_rel.shape[1]
    all_slots = slots * groups
    row_blocks = ent_rows // TILE
    own_bases = bases.shape[0]

    rel_hot = tile_rel[0][:, None] == jnp.arange(rel_count, dtype=jnp.int32)
    coef = jnp.dot(rel_hot.astype(F32), coeffs, precision=HIGH)
    alive = jnp.arange(slots, dtype=jnp.int32) < tile_live[0, 0]
    key = (g * rel_count + tile_rel[0]) * row_blocks + tile_row[0]
    lists = jnp.concatenate(
        [
            tile_edges[0].astype(F32),
            coef,
            key[:, None].astype(F32),
            alive[:, None].astype(F32),
            tile_row[0][:, None].astype(F32),
            tile_col[0][:, None].astype(F32),
        ],
        axis=1,
    )
    lists = lax.all_gather(lists, "rel", axis=0, tiled=True)
    listed = tile_edges.shape[2]
    edges = lists[:, :listed].astype(jnp.int32)
    meta = lists[:, listed:].T
    coef_all = meta[:bases_count]
    marks = meta[bases_count : bases_count + 2]
    spots = meta[bases_count + 2 :].astype(jnp.int32)
    lives = jnp.sum(marks[1].reshape(groups, slots), axis=1).astype(jnp.int32)
    spots = jnp.concatenate([spots, jnp.pad(lives, (0, all_slots - groups))[None]], axis=0)

    own = lax.dynamic_slice_in_dim(feats, g * share, share, 1)
    flat_rows = send_rows.reshape(-1)
    pick = (flat_rows[:, None] == jnp.arange(ent_rows, dtype=jnp.int32)).astype(BF16)
    outgoing = jnp.dot(pick, own, preferred_element_type=F32).astype(BF16)
    incoming = lax.all_to_all(outgoing, "ent", split_axis=0, concat_axis=0, tiled=True)
    extended = jnp.concatenate([own, incoming], axis=0)
    all_bases = lax.all_to_all(bases, "rel", split_axis=1, concat_axis=0, tiled=True)

    adj, inv = pl.pallas_call(
        tiles_kernel,
        out_shape=(
            jax.ShapeDtypeStruct((all_slots, TILE, TILE), BF16),
            jax.ShapeDtypeStruct((all_slots, TILE), F32),
        ),
        in_specs=[VMEM] * 2,
        out_specs=(VMEM, VMEM),
        scratch_shapes=[pltpu.VMEM((all_slots, TILE), F32)],
        compiler_params=pltpu.CompilerParams(vmem_limit_bytes=32 << 20),
    )(edges, marks)

    rows = extended.shape[0]
    cores = 2
    zs = ents // (cores * groups)
    lines = own_bases * share // (cores * zs)
    basis, own_grads, halo_grads, parts = pl.pallas_call(
        functools.partial(main_kernel, groups=groups),
        out_shape=(
            jax.ShapeDtypeStruct((cores, groups, zs, lines, width), BF16),
            jax.ShapeDtypeStruct((ent_rows, share), F32),
            jax.ShapeDtypeStruct((rows - ent_rows, share), BF16),
            jax.ShapeDtypeStruct((bases_count, all_slots), F32),
        ),
        in_specs=[SMEM, SMEM] + [VMEM] * 6,
        out_specs=(VMEM,) * 4,
        scratch_shapes=[
            pltpu.VMEM((bases_count, rows, ent_rows), F32),
            pltpu.VMEM((bases_count, share, ent_rows), BF16),
            pltpu.VMEM((rows, share), F32),
            pltpu.VMEM((bases_count, all_slots, TILE), F32),
        ],
        compiler_params=pltpu.CompilerParams(vmem_limit_bytes=56 << 20),
    )(spots, coef_all, adj, inv, extended, extended.T, cotangent, all_bases)

    padded = -(-rel_count // LANES) * LANES
    sems = pltpu.SemaphoreType.DMA
    return pl.pallas_call(
        share_kernel,
        out_shape=(
            jax.ShapeDtypeStruct((ent_rows, share), F32),
            jax.ShapeDtypeStruct((own_bases, lines // own_bases, width), F32),
            jax.ShapeDtypeStruct((rel_count, bases_count), F32),
        ),
        in_specs=[VMEM] * 6,
        out_specs=(VMEM,) * 3,
        scratch_shapes=[
            pltpu.VMEM((rows - ent_rows, share), BF16),
            pltpu.VMEM((groups, zs, lines, width), BF16),
            pltpu.VMEM((groups, zs, lines, width), BF16),
            pltpu.VMEM((groups, zs, lines, width), BF16),
            pltpu.VMEM((zs, lines, width), F32),
            pltpu.VMEM((zs, lines, width), BF16),
            pltpu.VMEM((zs, lines, width), BF16),
            pltpu.VMEM((own_bases, lines // own_bases, width), F32),
            pltpu.VMEM((groups, bases_count, all_slots), F32),
            pltpu.VMEM((2, bases_count, padded), F32),
            pltpu.VMEM((groups, bases_count, padded), F32),
            pltpu.VMEM((zs, bases_count, padded), F32),
            sems((2, ents)),
            sems((2, groups)),
            sems((2, groups)),
            sems((2, zs)),
            sems((2, 1)),
            sems((2, groups)),
            sems((2, 1)),
            sems((2, groups)),
            sems((2, zs)),
        ],
        compiler_params=pltpu.CompilerParams(
            collective_id=1, has_side_effects=True, vmem_limit_bytes=32 << 20
        ),
    )(basis, own_grads, halo_grads, flat_rows[None], parts, marks[:1].astype(jnp.int32) // row_blocks)


def solution(mesh):
    placed = (
        P("ent", None),
        P("ent", None),
        P("rel", None, None),
        P("rel", None),
        P("ent", None),
        P("ent", "rel"),
        P("ent", "rel"),
        P("ent", "rel"),
        P("ent", "rel", None),
        P("ent", "rel"),
    )
    return jax.shard_map(
        per_device,
        mesh=mesh,
        in_specs=placed,
        out_specs=(P("ent", "rel"), P("rel", "ent", None), P("rel", None)),
        check_vma=False,
    )
```

```python
import functools

import jax
import jax.numpy as jnp
from jax import lax
from jax.experimental import pallas as pl
from jax.experimental.pallas import tpu as pltpu
from jax.sharding import PartitionSpec as P

TILE = 128
LANES = 128
BF16 = jnp.bfloat16
F32 = jnp.float32
HIGH = lax.Precision.HIGHEST
VMEM = pl.BlockSpec(memory_space=pltpu.VMEM)
SMEM = pl.BlockSpec(memory_space=pltpu.SMEM)


def gather_kernel(
    feats_ref,
    bases_ref,
    coeffs_ref,
    send_ref,
    rel_ref,
    row_ref,
    col_ref,
    edges_ref,
    live_ref,
    adj_out,
    inv_out,
    cols_out,
    bases_out,
    spots_out,
    coef_out,
    key_out,
    rows_out,
    halo_out,
    halo_in,
    lists_in,
    meta_in,
    sums_ref,
    halo_sems,
    bases_sems,
    lists_sems,
    meta_sems,
):
    d, y = lax.axis_index("ent"), lax.axis_index("rel")
    groups = lists_in.shape[0]
    _, slots, listed = edges_ref.shape
    all_slots = groups * slots
    ents, peer_rows = send_ref.shape
    ent_rows = feats_ref.shape[0]
    own_bases = bases_ref.shape[0]
    share = halo_in.shape[1]
    rel_count, bases_count = coeffs_ref.shape
    halo_rows = ents * peer_rows

    barrier = pltpu.get_barrier_semaphore()

    def greet(to_ent, to_rel):
        pl.semaphore_signal(
            barrier, inc=1, device_id=(to_ent, to_rel), device_id_type=pl.DeviceIdType.MESH
        )

    for k in range(1, groups):
        greet(d, lax.rem(y + k, groups))

    def greet_ent(off, carry):
        greet(lax.rem(d + off, ents), y)
        return carry

    lax.fori_loop(1, ents, greet_ent, 0)

    def send(src, dst, sems, at, to_ent, to_rel):
        return pltpu.make_async_remote_copy(
            src_ref=src,
            dst_ref=dst,
            send_sem=sems.at[0, at],
            recv_sem=sems.at[1, at],
            device_id=(to_ent, to_rel),
            device_id_type=pl.DeviceIdType.MESH,
        )

    lane = lax.broadcasted_iota(jnp.int32, (slots, all_slots), 1)
    slot = lax.broadcasted_iota(jnp.int32, (slots, all_slots), 0)
    spread = jnp.where(lane == slot + y * slots, 1.0, 0.0)

    def at_lanes(values):
        return jnp.dot(values, spread, preferred_element_type=F32, precision=HIGH)

    order = lax.broadcasted_iota(jnp.int32, (1, slots), 1)
    alive = jnp.where(order < live_ref[...], 1.0, 0.0)
    rel = rel_ref[...]
    marks = jnp.concatenate(
        [
            (rel + y * rel_count).astype(F32),
            row_ref[...].astype(F32),
            col_ref[...].astype(F32),
            alive,
            jnp.zeros((4, slots), F32),
        ],
        axis=0,
    )
    rel_hot = jnp.where(
        lax.broadcasted_iota(jnp.int32, (rel_count, slots), 0) == rel, 1.0, 0.0
    )
    coef = lax.dot_general(
        coeffs_ref[...].T, rel_hot, (((1,), (0,)), ((), ())), preferred_element_type=F32, precision=HIGH
    )
    meta_in[y] = at_lanes(jnp.concatenate([marks, coef], axis=0))

    own_at = pl.ds(pl.multiple_of(y * share, share), share)
    own = feats_ref[:, own_at].astype(F32)
    blocks = [own[i * TILE : (i + 1) * TILE, :].T.astype(BF16) for i in range(ent_rows // TILE)]
    for i, one in enumerate(blocks):
        cols_out[i] = one
    own_t = jnp.concatenate(blocks, axis=1)
    spot = lax.broadcasted_iota(jnp.int32, (peer_rows, halo_rows), 1)
    inside = lax.broadcasted_iota(jnp.int32, (peer_rows, halo_rows), 0)
    fan = jnp.where(lax.rem(spot, peer_rows) == inside, 1.0, 0.0)
    fanned = jnp.dot(
        send_ref[...].astype(F32), fan, preferred_element_type=F32, precision=HIGH
    )
    spot = lax.broadcasted_iota(jnp.int32, (ents, halo_rows), 1)
    peer = lax.broadcasted_iota(jnp.int32, (ents, halo_rows), 0)
    flat = jnp.sum(
        jnp.where(lax.div(spot, peer_rows) == peer, fanned, 0.0), axis=0, keepdims=True
    ).astype(jnp.int32)
    rows_out[...] = flat
    row = lax.broadcasted_iota(jnp.int32, (ent_rows, TILE), 0)
    for i in range(halo_rows // TILE):
        hot = jnp.where(row == flat[:, i * TILE : (i + 1) * TILE], 1.0, 0.0).astype(BF16)
        picked = jnp.dot(own_t, hot, preferred_element_type=F32)
        halo_out[i * TILE : (i + 1) * TILE, :] = picked.T.astype(BF16)

    pl.semaphore_wait(barrier, ents - 1 + groups - 1)

    rel_copies = []
    for k in range(1, groups):
        to = lax.rem(y + k, groups)
        rel_copies.append(
            (
                send(edges_ref.at[0], lists_in.at[y], lists_sems, k, d, to),
                send(meta_in.at[y], meta_in.at[y], meta_sems, k, d, to),
            )
        )
    for pair in rel_copies:
        for copy in pair:
            copy.start()

    def halo_copy(off):
        to = lax.rem(d + off, ents)
        return send(
            halo_out.at[pl.ds(pl.multiple_of(to * peer_rows, peer_rows), peer_rows), :],
            halo_in.at[pl.ds(pl.multiple_of(d * peer_rows, peer_rows), peer_rows), :],
            halo_sems,
            off,
            to,
            y,
        )

    def halo_start(off, carry):
        halo_copy(off).start()
        return carry

    lax.fori_loop(1, ents, halo_start, 0)
    bases_copies = []
    for k in (2, 1, 3):
        to = lax.rem(y + k, groups)
        copy = send(
            bases_ref.at[:, pl.ds(pl.multiple_of(to * share, share), share), :],
            bases_out.at[pl.ds(y * own_bases, own_bases)],
            bases_sems,
            k,
            d,
            to,
        )
        copy.start()
        bases_copies.append(copy)
    bases_out[pl.ds(y * own_bases, own_bases)] = bases_ref[:, own_at, :]
    mine = pl.ds(pl.multiple_of(d * peer_rows, peer_rows), peer_rows)
    halo_in[mine, :] = halo_out[mine, :]

    lists_in[y] = edges_ref[0]
    place = lax.broadcasted_iota(jnp.int32, (TILE, listed), 0).astype(BF16)
    for k in range(groups):
        if k:
            for copy in rel_copies[groups - 1 - k]:
                copy.wait()
        group = lax.rem(y + k, groups)

        def build(i, carry, group=group):
            edge = lists_in[group, pl.ds(i, 1), :]
            to_col = (edge & (TILE - 1)).astype(BF16)
            to_row = (edge >> 7).astype(BF16)
            one, zero = jnp.ones((), BF16), jnp.zeros((), BF16)
            col_hot = jnp.where(place == to_col, one, zero)
            row_hot = jnp.where(place == to_row, one, zero)
            counts = lax.dot_general(
                col_hot, row_hot, (((1,), (1,)), ((), ())), preferred_element_type=F32
            )
            t = group * slots + i
            adj_out[t] = counts.astype(BF16)
            sums_ref[pl.ds(t, 1), :] = jnp.sum(counts, axis=0, keepdims=True)
            return carry

        lax.fori_loop(0, slots, build, 0, unroll=4)

    meta = meta_in[0]
    for k in range(1, groups):
        meta = meta + meta_in[k]
    key = jnp.broadcast_to(meta[0:1] * (ent_rows // TILE) + meta[1:2], (all_slots, all_slots))
    live = jnp.broadcast_to(meta[3:4], (all_slots, all_slots))
    same = jnp.where(key == key.T, live, 0.0).astype(BF16)
    degree = jnp.dot(same, sums_ref[...].astype(BF16), preferred_element_type=F32)
    inv_out[...] = live.T / jnp.maximum(degree, 1.0)
    key_out[...] = meta[0:1].astype(jnp.int32)
    coef_out[...] = meta[8 : 8 + bases_count]
    counted = [
        jnp.broadcast_to(
            jnp.sum(meta[3:4, g * slots : (g + 1) * slots], axis=1, keepdims=True), (1, all_slots)
        )
        for g in range(groups)
    ]
    spots_out[...] = jnp.concatenate([meta[1:3], *counted, jnp.zeros((2, all_slots), F32)], axis=0).astype(
        jnp.int32
    )

    def halo_wait(off, carry):
        halo_copy(off).wait()
        return carry

    lax.fori_loop(1, ents, halo_wait, 0)
    for i in range(halo_rows // TILE):
        cols_out[ent_rows // TILE + i] = (
            halo_in[i * TILE : (i + 1) * TILE, :].astype(F32).T.astype(BF16)
        )
    for copy in bases_copies:
        copy.wait()


def main_kernel(
    spots_ref,
    coef_ref,
    adj_ref,
    inv_ref,
    cols_ref,
    cot_ref,
    bases_ref,
    basis_ref,
    own_ref,
    halo_ref,
    parts_ref,
    dm_ref,
    mixed_ref,
    y_ref,
    z_ref,
    grads_ref,
    inner_ref,
    *,
    groups,
    step,
):
    row_blocks, bases_count = dm_ref.shape[:2]
    slots = adj_ref.shape[0]
    per_group = slots // groups
    cores, pairs, zs, lines, width = basis_ref.shape
    each = bases_count // pairs
    strip = lines // each

    def over_tiles(body):
        for g in range(groups):

            def some(n, carry, g=g):
                for i in range(step):
                    body(g * per_group + n * step + i)
                return carry

            lax.fori_loop(0, lax.div(spots_ref[2 + g, 0] + step - 1, step), some, 0)

    def gather(t):
        y = jnp.dot(cols_ref[spots_ref[1, t]], adj_ref[t], preferred_element_type=F32)
        y_ref[t] = y * inv_ref[pl.ds(t, 1), :]

    over_tiles(gather)

    def prepare(b, carry):
        dm = lax.dot_general(
            bases_ref[b], cot_ref[...], (((1,), (1,)), ((), ())), preferred_element_type=F32
        )
        for k in range(row_blocks):
            dm_ref[k, b] = dm[:, k * TILE : (k + 1) * TILE].astype(BF16).astype(F32)
            mixed_ref[k, b] = jnp.zeros((TILE, TILE), F32)
        return carry

    lax.fori_loop(0, bases_count, prepare, 0)
    inner_ref[...] = jnp.zeros_like(inner_ref)

    def weigh(t, carry):
        k = spots_ref[0, t]
        y = y_ref[t]
        z = jnp.zeros_like(y)
        for b in range(bases_count):
            c = coef_ref[b, t]
            dm = dm_ref[k, b]
            mixed_ref[k, b] += c * y
            inner_ref[b, pl.ds(t, 1), :] = jnp.sum(y * dm, axis=0, keepdims=True)
            z = z + c * dm
        z_ref[t] = (z * inv_ref[pl.ds(t, 1), :]).astype(BF16)
        return carry

    for g in range(groups):
        lax.fori_loop(g * per_group, g * per_group + spots_ref[2 + g, 0], weigh, 0)
    for g in range(groups):

        def fill(t, carry):
            z_ref[t] = jnp.zeros(z_ref.shape[1:], BF16)
            return carry

        used = spots_ref[2 + g, 0]
        upto = lax.div(used + step - 1, step) * step
        lax.fori_loop(g * per_group + used, g * per_group + upto, fill, 0)

    grads_ref[...] = jnp.zeros_like(grads_ref)

    def scatter(t):
        back = lax.dot_general(
            adj_ref[t], z_ref[t], (((1,), (1,)), ((), ())), preferred_element_type=F32
        )
        grads_ref[spots_ref[1, t]] += back

    over_tiles(scatter)

    def outer(pair, carry):
        results = []
        for one in range(each):
            b = pair * each + one
            mixed = jnp.concatenate([mixed_ref[k, b] for k in range(row_blocks)], axis=1)
            results.append(
                jnp.dot(mixed.astype(BF16), cot_ref[...], preferred_element_type=F32)
            )
        for z in range(zs):
            for core in range(cores):
                at = (z * cores + core) * strip
                basis_ref[core, pair, z] = jnp.concatenate(
                    [r[at : at + strip] for r in results], axis=0
                ).astype(BF16)
        return carry

    lax.fori_loop(0, pairs, outer, 0)
    for i in range(grads_ref.shape[0]):
        at = i * TILE
        if i < row_blocks:
            own_ref[at : at + TILE, :] = grads_ref[i]
        else:
            at -= row_blocks * TILE
            halo_ref[at : at + TILE, :] = grads_ref[i].astype(BF16)
    for b in range(bases_count):
        parts_ref[pl.ds(b, 1), :] = jnp.sum(inner_ref[b].T, axis=0, keepdims=True)


def share_kernel(
    basis_ref,
    own_ref,
    halo_ref,
    rows_ref,
    parts_ref,
    key_ref,
    grads_out,
    basis_out,
    coeff_out,
    back_ref,
    core_in,
    x_out,
    x_in,
    x_sum,
    z_out,
    z_in,
    final_ref,
    c_rel,
    c_core,
    c_x,
    c_z,
    halo_sems,
    core_sems,
    x_sems,
    z_sems,
    swap_sems,
    c_rel_sems,
    c_core_sems,
    c_x_sems,
    c_z_sems,
):
    cores, xs, zs, lines, width = basis_ref.shape
    ents = cores * xs * zs
    peer_rows = halo_ref.shape[0] // ents
    groups = xs
    d, y = lax.axis_index("ent"), lax.axis_index("rel")
    core = lax.rem(d, cores)
    z = lax.rem(lax.div(d, cores), zs)
    x = lax.div(d, cores * zs)

    def ent(x_at, z_at, core_at):
        return (x_at * zs + z_at) * cores + core_at

    def send(src, dst, sems, at, to_ent, to_rel):
        return pltpu.make_async_remote_copy(
            src_ref=src,
            dst_ref=dst,
            send_sem=sems.at[0, at],
            recv_sem=sems.at[1, at],
            device_id=(to_ent, to_rel),
            device_id_type=pl.DeviceIdType.MESH,
        )

    barrier = pltpu.get_barrier_semaphore()

    def greet(to_ent, to_rel):
        pl.semaphore_signal(
            barrier, inc=1, device_id=(to_ent, to_rel), device_id_type=pl.DeviceIdType.MESH
        )

    def greet_ent(off, carry):
        greet(lax.rem(d + off, ents), y)
        return carry

    lax.fori_loop(1, ents, greet_ent, 0)
    for k in range(1, groups):
        greet(d, lax.rem(y + k, groups))
    other = ent(y, z, core)

    @pl.when(x != y)
    def _():
        greet(other, x)

    pl.semaphore_wait(barrier, ents - 1 + groups - 1 + jnp.where(x != y, 1, 0))

    c_rel_copies = [
        send(parts_ref, c_rel.at[k], c_rel_sems, k, d, lax.rem(y + k, groups))
        for k in range(1, groups)
    ]
    for copy in c_rel_copies:
        copy.start()
    order = (2, 1, 3, 0)
    mate = d + 1 - 2 * core
    core_copies = {}
    for k in order:
        to_x = lax.rem(x + k, xs)
        core_copies[k] = send(
            basis_ref.at[1 - core, to_x], core_in.at[k], core_sems, k, mate, y
        )
        core_copies[k].start()

    def halo_copy(off):
        to = lax.rem(d + off, ents)
        return send(
            halo_ref.at[pl.ds(pl.multiple_of(to * peer_rows, peer_rows), peer_rows), :],
            back_ref.at[pl.ds(pl.multiple_of(d * peer_rows, peer_rows), peer_rows), :],
            halo_sems,
            off,
            to,
            y,
        )

    def halo_start(off, carry):
        halo_copy(off).start()
        return carry

    lax.fori_loop(1, ents, halo_start, 0)
    mine = pl.ds(pl.multiple_of(d * peer_rows, peer_rows), peer_rows)
    back_ref[mine, :] = halo_ref[mine, :]

    total = parts_ref[...]
    for k in range(1, groups):
        c_rel_copies[k - 1].wait()
        total = total + c_rel[k]
    rel_count = coeff_out.shape[0]
    slots = key_ref.shape[1]
    padded = c_core.shape[2]
    relation = lax.broadcasted_iota(jnp.int32, (padded, slots), 0) + y * rel_count
    hot = jnp.where(relation == key_ref[...], 1.0, 0.0)
    by_relation = lax.dot_general(
        total, hot, (((1,), (1,)), ((), ())), preferred_element_type=F32, precision=HIGH
    )
    c_core[0] = by_relation
    c_core_copy = send(c_core.at[0], c_core.at[1], c_core_sems, 0, mate, y)
    c_core_copy.start()

    x_copies = {}
    for k in order:
        core_copies[k].wait()
        to_x = lax.rem(x + k, xs)
        value = basis_ref[core, to_x].astype(F32) + core_in[k].astype(F32)
        if k == 0:
            x_sum[...] = value
        else:
            x_out[k] = value.astype(BF16)
            x_copies[k] = send(
                x_out.at[k], x_in.at[k], x_sems, k, ent(to_x, z, core), y
            )
            x_copies[k].start()

    c_core_copy.wait()
    c_x[x] = c_core[0] + c_core[1]
    c_x_copies = [
        send(c_x.at[x], c_x.at[x], c_x_sems, k, ent(lax.rem(x + k, xs), z, core), y)
        for k in range(1, xs)
    ]
    for copy in c_x_copies:
        copy.start()

    for k in range(1, xs):
        x_copies[k].wait()
    z_copies = []
    for k in range(1, zs):
        to_z = lax.rem(z + k, zs)
        value = x_sum[to_z]
        for j in range(1, xs):
            value = value + x_in[j, to_z].astype(F32)
        z_out[k] = value.astype(BF16)
        copy = send(z_out.at[k], z_in.at[k], z_sems, k, ent(x, to_z, core), y)
        copy.start()
        z_copies.append(copy)
    value = x_sum[z]
    for j in range(1, xs):
        value = value + x_in[j, z].astype(F32)

    for copy in c_x_copies:
        copy.wait()
    total = c_x[0]
    for j in range(1, xs):
        total = total + c_x[j]
    c_z[z] = total
    c_z_copies = [
        send(c_z.at[z], c_z.at[z], c_z_sems, k, ent(x, lax.rem(z + k, zs), core), y)
        for k in range(1, zs)
    ]
    for copy in c_z_copies:
        copy.start()

    for k in range(1, zs):
        z_copies[k - 1].wait()
        value = value + z_in[k].astype(F32)
    final_ref[...] = value.reshape(final_ref.shape)
    swap = send(final_ref, basis_out, swap_sems, 0, other, x)

    @pl.when(x != y)
    def _():
        swap.start()

    def halo_wait(off, carry):
        halo_copy(off).wait()
        return carry

    lax.fori_loop(1, ents, halo_wait, 0)
    ent_rows = own_ref.shape[0]
    returned = back_ref.shape[0]
    step = 256
    for at in range(0, returned, step):
        row = lax.broadcasted_iota(jnp.int32, (ent_rows, step), 0)
        hot = jnp.where(row == rows_ref[:, at : at + step], 1.0, 0.0).astype(BF16)
        more = jnp.dot(hot, back_ref[at : at + step, :], preferred_element_type=F32)
        base = own_ref[...] if at == 0 else grads_out[...]
        grads_out[...] = base + more

    for copy in c_z_copies:
        copy.wait()
    total = c_z[0]
    for j in range(1, zs):
        total = total + c_z[j]
    coeff_out[...] = total.T[:rel_count, :]

    @pl.when(x != y)
    def _():
        swap.wait()

    @pl.when(x == y)
    def _():
        basis_out[...] = final_ref[...]


def per_device(
    feats, cotangent, bases, coeffs, send_rows, tile_rel, tile_row, tile_col, tile_edges, tile_live
):
    ent_rows, width = feats.shape
    groups = lax.axis_size("rel")
    ents = lax.axis_size("ent")
    share = width // groups
    rel_count, bases_count = coeffs.shape
    slots = tile_rel.shape[1]
    all_slots = slots * groups
    row_blocks = ent_rows // TILE
    own_bases = bases.shape[0]
    halo_rows = send_rows.size
    col_blocks = (ent_rows + halo_rows) // TILE
    listed = tile_edges.shape[2]
    sems = pltpu.SemaphoreType.DMA
    shape = jax.ShapeDtypeStruct
    adj, inv, columns, all_bases, spots, coef, key, flat_rows = pl.pallas_call(
        gather_kernel,
        out_shape=(
            shape((all_slots, TILE, TILE), BF16),
            shape((all_slots, TILE), F32),
            shape((col_blocks, share, TILE), BF16),
            shape((bases_count, share, width), BF16),
            shape((8, all_slots), jnp.int32),
            shape((bases_count, all_slots), F32),
            shape((1, all_slots), jnp.int32),
            shape((1, halo_rows), jnp.int32),
        ),
        in_specs=[VMEM] * 9,
        out_specs=(VMEM,) * 8,
        scratch_shapes=[
            pltpu.VMEM((halo_rows, share), BF16),
            pltpu.VMEM((halo_rows, share), BF16),
            pltpu.VMEM((groups, slots, listed), jnp.int32),
            pltpu.VMEM((groups, 8 + bases_count, all_slots), F32),
            pltpu.VMEM((all_slots, TILE), F32),
            sems((2, ents)),
            sems((2, groups)),
            sems((2, groups)),
            sems((2, groups)),
        ],
        compiler_params=pltpu.CompilerParams(
            collective_id=0, has_side_effects=True, vmem_limit_bytes=40 << 20
        ),
    )(feats, bases, coeffs, send_rows, tile_rel, tile_row, tile_col, tile_edges, tile_live)

    cores = 2
    zs = ents // (cores * groups)
    lines = own_bases * share // (cores * zs)
    basis, own_grads, halo_grads, parts = pl.pallas_call(
        functools.partial(main_kernel, groups=groups, step=4),
        out_shape=(
            shape((cores, groups, zs, lines, width), BF16),
            shape((ent_rows, share), F32),
            shape((halo_rows, share), BF16),
            shape((bases_count, all_slots), F32),
        ),
        in_specs=[SMEM, SMEM] + [VMEM] * 5,
        out_specs=(VMEM,) * 4,
        scratch_shapes=[
            pltpu.VMEM((row_blocks, bases_count, share, TILE), F32),
            pltpu.VMEM((row_blocks, bases_count, share, TILE), F32),
            pltpu.VMEM((all_slots, share, TILE), F32),
            pltpu.VMEM((all_slots, share, TILE), BF16),
            pltpu.VMEM((col_blocks, TILE, share), F32),
            pltpu.VMEM((bases_count, all_slots, TILE), F32),
        ],
        compiler_params=pltpu.CompilerParams(vmem_limit_bytes=48 << 20),
    )(spots, coef, adj, inv, columns, cotangent, all_bases)

    padded = -(-rel_count // LANES) * LANES
    return pl.pallas_call(
        share_kernel,
        out_shape=(
            jax.ShapeDtypeStruct((ent_rows, share), F32),
            jax.ShapeDtypeStruct((own_bases, lines // own_bases, width), F32),
            jax.ShapeDtypeStruct((rel_count, bases_count), F32),
        ),
        in_specs=[VMEM] * 6,
        out_specs=(VMEM,) * 3,
        scratch_shapes=[
            pltpu.VMEM((halo_rows, share), BF16),
            pltpu.VMEM((groups, zs, lines, width), BF16),
            pltpu.VMEM((groups, zs, lines, width), BF16),
            pltpu.VMEM((groups, zs, lines, width), BF16),
            pltpu.VMEM((zs, lines, width), F32),
            pltpu.VMEM((zs, lines, width), BF16),
            pltpu.VMEM((zs, lines, width), BF16),
            pltpu.VMEM((own_bases, lines // own_bases, width), F32),
            pltpu.VMEM((groups, bases_count, all_slots), F32),
            pltpu.VMEM((2, bases_count, padded), F32),
            pltpu.VMEM((groups, bases_count, padded), F32),
            pltpu.VMEM((zs, bases_count, padded), F32),
            sems((2, ents)),
            sems((2, groups)),
            sems((2, groups)),
            sems((2, zs)),
            sems((2, 1)),
            sems((2, groups)),
            sems((2, 1)),
            sems((2, groups)),
            sems((2, zs)),
        ],
        compiler_params=pltpu.CompilerParams(
            collective_id=1, has_side_effects=True, vmem_limit_bytes=32 << 20
        ),
    )(basis, own_grads, halo_grads, flat_rows, parts, key)


def solution(mesh):
    placed = (
        P("ent", None),
        P("ent", None),
        P("rel", None, None),
        P("rel", None),
        P("ent", None),
        P("ent", "rel"),
        P("ent", "rel"),
        P("ent", "rel"),
        P("ent", "rel", None),
        P("ent", "rel"),
    )
    return jax.shard_map(
        per_device,
        mesh=mesh,
        in_specs=placed,
        out_specs=(P("ent", "rel"), P("rel", "ent", None), P("rel", None)),
        check_vma=False,
    )
```

```python
import jax
import jax.numpy as jnp
from jax import lax
from jax.experimental import pallas as pl
from jax.experimental.pallas import tpu as pltpu
from jax.sharding import PartitionSpec as P

TILE = 128
LANES = 128
BF16 = jnp.bfloat16
F32 = jnp.float32
HIGH = lax.Precision.HIGHEST
VMEM = pl.BlockSpec(memory_space=pltpu.VMEM)
HBM = pl.BlockSpec(memory_space=pltpu.HBM)
STEP = 4


def lanes_to(value, count):
    return jnp.broadcast_to(value, (count, value.shape[1]))


def arrange(meta, row_blocks, places):
    tiles = meta.shape[1]
    key, row, col, live = meta[0:1], meta[1:2], meta[2:3], meta[3:4]
    earlier = lax.broadcasted_iota(jnp.int32, (tiles, tiles), 0) < lax.broadcasted_iota(
        jnp.int32, (tiles, tiles), 1
    )
    at = lax.broadcasted_iota(jnp.int32, (1, places), 1).astype(F32)
    spot = lax.broadcasted_iota(jnp.int32, (tiles, places), 1).astype(F32)
    name = lax.broadcasted_iota(jnp.int32, (tiles, places), 0).astype(F32)

    def down(value):
        turned = lanes_to(value, tiles).T
        return jnp.concatenate([turned] * (places // tiles), axis=1)

    rows, cols = lanes_to(row, tiles), lanes_to(col, tiles)
    rows_d, cols_d, live_d = down(row), down(col), down(live)

    def count(mask):
        return jnp.sum(jnp.where(mask, live_d[:, :tiles], 0.0), axis=0, keepdims=True)

    before_row = count((rows_d[:, :tiles] == rows) & earlier)
    before_col = count((cols_d[:, :tiles] == cols) & earlier)
    lower_col = count(cols_d[:, :tiles] < cols)
    start = jnp.zeros((1, 1), F32)
    by_row, block = before_row, jnp.zeros_like(at)
    last, filled = jnp.zeros_like(at), jnp.zeros_like(at)
    for k in range(row_blocks):
        held = jnp.sum(jnp.where(row == k, live, 0.0), axis=1, keepdims=True)
        filled = filled + jnp.where(at == k, jnp.where(held > 0, 1.0, 0.0), 0.0)
        start = start + jnp.floor((held + (STEP - 1)) * (1.0 / STEP)) * STEP
        if k < row_blocks - 1:
            last = last + jnp.where(at == k, jnp.maximum(start * (1.0 / STEP) - 1.0, 0.0), 0.0)
            block = block + jnp.where(at >= start, 1.0, 0.0)
            by_row = by_row + jnp.where(row > k, jnp.where(row == k + 1, start, 0.0), 0.0)
    by_row = jnp.where(live > 0, by_row, -1.0)
    by_col = jnp.where(live > 0, lower_col + before_col, -1.0)
    row_hot = jnp.where(down(by_row) == spot, 1.0, 0.0)
    col_hot = jnp.where(down(by_col) == spot, 1.0, 0.0)

    def pick(hot, value, empty):
        return jnp.sum(hot * (value - empty), axis=0, keepdims=True) + empty

    upto = jnp.sum(jnp.where(cols_d <= spot, live_d, 0.0), axis=0, keepdims=True)
    own = jnp.sum(jnp.where(cols_d == spot, live_d, 0.0), axis=0, keepdims=True)
    spots = [
        pick(row_hot, name, float(tiles)),
        block,
        jnp.concatenate([col, jnp.zeros((1, places - tiles), F32)], axis=1),
        pick(col_hot, name, float(tiles)),
        pick(col_hot, down(by_row), 0.0),
        pick(col_hot, down(jnp.where(before_col > 0, 1.0, 0.0)), 0.0),
        jnp.maximum(upto - 1.0, 0.0),
        jnp.where(own > 0, 1.0, 0.0),
        last,
        filled,
        jnp.zeros((6, places), F32),
    ]
    coef = jnp.dot(meta[8:16], row_hot, preferred_element_type=F32, precision=HIGH)
    keys = pick(row_hot, down(key), -1.0)
    return jnp.concatenate(spots, axis=0).astype(jnp.int32), coef, keys.astype(jnp.int32), by_row


def whole_kernel(
    feats_hbm,
    cot_hbm,
    bases_hbm,
    coeffs_hbm,
    send_hbm,
    rel_hbm,
    row_hbm,
    col_hbm,
    edges_hbm,
    live_hbm,
    grads_out,
    basis_out,
    coeff_out,
    feats_ref,
    cot_ref,
    bases_ref,
    coeffs_ref,
    send_ref,
    rel_ref,
    row_ref,
    col_ref,
    live_ref,
    lists_ref,
    meta_ref,
    sums_ref,
    adj_ref,
    inv_ref,
    cols_ref,
    spots_vmem,
    coef_vmem,
    spots_ref,
    coef_ref,
    y_ref,
    runs_ref,
    z_ref,
    dm_ref,
    basis_ref,
    inner_ref,
    parts_ref,
    hot_ref,
    halo_out,
    halo_in,
    back_out,
    back_in,
    core_in,
    x_out,
    x_in,
    x_sum,
    z_out,
    z_in,
    final_ref,
    c_rel,
    c_core,
    c_x,
    c_z,
    load_sems,
    halo_sems,
    bases_sems,
    mate_sems,
    lists_sems,
    meta_sems,
    back_sems,
    core_sems,
    x_sems,
    z_sems,
    swap_sems,
    c_rel_sems,
    c_core_sems,
    c_x_sems,
    c_z_sems,
):
    cores, xs, zs, lines, width = basis_ref.shape
    groups = xs
    ents = cores * xs * zs
    d, y = lax.axis_index("ent"), lax.axis_index("rel")
    core = lax.rem(d, cores)
    z = lax.rem(lax.div(d, cores), zs)
    x = lax.div(d, cores * zs)
    mate = d + 1 - 2 * core
    all_slots, listed = lists_ref.shape
    slots = all_slots // groups
    peer_rows = send_ref.shape[0]
    ent_rows, share = feats_ref.shape
    row_blocks = ent_rows // TILE
    bases_count, rel_count = coeffs_ref.shape
    own_bases = bases_count // groups
    halo_rows = ents * peer_rows
    places = y_ref.shape[0]
    steps = places // STEP
    own_at = pl.ds(pl.multiple_of(y * share, share), share)
    own_slots = pl.ds(pl.multiple_of(y * slots, slots), slots)

    loads = [
        pltpu.make_async_copy(src, dst, load_sems.at[i])
        for i, (src, dst) in enumerate(
            (
                (rel_hbm, rel_ref),
                (row_hbm, row_ref),
                (col_hbm, col_ref),
                (live_hbm, live_ref),
                (coeffs_hbm, coeffs_ref),
                (edges_hbm.at[0], lists_ref.at[own_slots, :]),
                (send_hbm, send_ref),
                (feats_hbm.at[:, own_at], feats_ref),
                (bases_hbm.at[:, own_at, :], bases_ref.at[pl.ds(y * own_bases, own_bases)]),
                (cot_hbm, cot_ref),
            )
        )
    ]
    for load in loads:
        load.start()

    def ent(x_at, z_at, core_at):
        return (x_at * zs + z_at) * cores + core_at

    def send(src, dst, sems, at, to_ent, to_rel):
        return pltpu.make_async_remote_copy(
            src_ref=src,
            dst_ref=dst,
            send_sem=sems.at[0, at],
            recv_sem=sems.at[1, at],
            device_id=(to_ent, to_rel),
            device_id_type=pl.DeviceIdType.MESH,
        )

    barrier = pltpu.get_barrier_semaphore()

    def greet(to_ent, to_rel):
        pl.semaphore_signal(
            barrier, inc=1, device_id=(to_ent, to_rel), device_id_type=pl.DeviceIdType.MESH
        )

    for k in range(1, groups):
        greet(d, lax.rem(y + k, groups))
    other = ent(y, z, core)

    @pl.when(x != y)
    def _():
        greet(other, x)

    def greet_ent(off, carry):
        greet(lax.rem(d + off, ents), y)
        return carry

    lax.fori_loop(1, ents, greet_ent, 0)

    lane = lax.broadcasted_iota(jnp.int32, (slots, all_slots), 1)
    slot = lax.broadcasted_iota(jnp.int32, (slots, all_slots), 0)
    spread = jnp.where(lane == slot + y * slots, 1.0, 0.0)
    for load in loads[:7]:
        load.wait()
    order = lax.broadcasted_iota(jnp.int32, (1, slots), 1)
    alive = jnp.where(order < live_ref[...], 1.0, 0.0)
    rel = rel_ref[...]
    marks = jnp.concatenate(
        [
            (rel + y * rel_count).astype(F32),
            row_ref[...].astype(F32),
            col_ref[...].astype(F32),
            alive,
            jnp.zeros((4, slots), F32),
        ],
        axis=0,
    )
    rel_hot = jnp.where(
        lax.broadcasted_iota(jnp.int32, (rel_count, slots), 0) == rel, 1.0, 0.0
    )
    coef = jnp.dot(coeffs_ref[...], rel_hot, preferred_element_type=F32, precision=HIGH)
    meta_ref[y] = jnp.dot(
        jnp.concatenate([marks, coef], axis=0), spread, preferred_element_type=F32, precision=HIGH
    )

    spot = lax.broadcasted_iota(jnp.int32, (ents, halo_rows), 1)
    peer = lax.broadcasted_iota(jnp.int32, (ents, halo_rows), 0)
    fan = jnp.where(lax.div(spot, peer_rows) == peer, 1.0, 0.0)
    fanned = jnp.dot(
        send_ref[...].astype(F32), fan, preferred_element_type=F32, precision=HIGH
    )
    spot = lax.broadcasted_iota(jnp.int32, (peer_rows, halo_rows), 1)
    inside = lax.broadcasted_iota(jnp.int32, (peer_rows, halo_rows), 0)
    flat = jnp.sum(
        jnp.where(lax.rem(spot, peer_rows) == inside, fanned, 0.0), axis=0, keepdims=True
    ).astype(jnp.int32)
    loads[7].wait()
    own = feats_ref[...].astype(F32)
    blocks = [own[i * TILE : (i + 1) * TILE, :].T.astype(BF16) for i in range(ent_rows // TILE)]
    for i, one in enumerate(blocks):
        cols_ref[i] = one
    own_t = jnp.concatenate(blocks, axis=1)
    row = lax.broadcasted_iota(jnp.int32, (ent_rows, TILE), 0)
    for i in range(halo_rows // TILE):
        hot = jnp.where(row == flat[:, i * TILE : (i + 1) * TILE], 1.0, 0.0).astype(BF16)
        picked = jnp.dot(own_t, hot, preferred_element_type=F32)
        halo_out[i * TILE : (i + 1) * TILE, :] = picked.T.astype(BF16)


    place = lax.broadcasted_iota(jnp.int32, (TILE, listed), 0).astype(BF16)

    def build_group(group):
        def build(i, carry):
            t = group * slots + i
            edge = lists_ref[pl.ds(t, 1), :]
            to_col = (edge & (TILE - 1)).astype(BF16)
            to_row = (edge >> 7).astype(BF16)
            one, zero = jnp.ones((), BF16), jnp.zeros((), BF16)
            col_hot = jnp.where(place == to_col, one, zero)
            row_hot = jnp.where(place == to_row, one, zero)
            counts = lax.dot_general(
                col_hot, row_hot, (((1,), (1,)), ((), ())), preferred_element_type=F32
            )
            adj_ref[t] = counts.astype(BF16)
            sums_ref[pl.ds(t, 1), :] = jnp.sum(counts, axis=0, keepdims=True)
            return carry

        lax.fori_loop(0, slots, build, 0, unroll=4)

    pl.semaphore_wait(barrier, ents - 1 + groups - 1 + jnp.where(x != y, 1, 0))

    rel_copies, bases_copies = [], []
    for k in range(1, groups):
        to = lax.rem(y + k, groups)
        rel_copies.append(
            (
                send(meta_ref.at[y], meta_ref.at[y], meta_sems, k, d, to),
                send(lists_ref.at[own_slots, :], lists_ref.at[own_slots, :], lists_sems, k, d, to),
            )
        )
        bases_copies.append(
            send(
                bases_hbm.at[core, pl.ds(pl.multiple_of(to * share, share), share), :],
                bases_ref.at[y * own_bases + core],
                bases_sems,
                k,
                d,
                to,
            )
        )
    for pair in rel_copies:
        for copy in pair:
            copy.start()
    for copy in bases_copies:
        copy.start()

    def exchange(src, dst, sems):
        def of(off):
            to = lax.rem(d + off, ents)
            return send(
                src.at[pl.ds(pl.multiple_of(to * peer_rows, peer_rows), peer_rows), :],
                dst.at[pl.ds(pl.multiple_of(d * peer_rows, peer_rows), peer_rows), :],
                sems,
                off,
                to,
                y,
            )

        def start(off, carry):
            of(off).start()
            return carry

        def wait(off, carry):
            of(off).wait()
            return carry

        def begin():
            lax.fori_loop(1, ents, start, 0)
            mine = pl.ds(pl.multiple_of(d * peer_rows, peer_rows), peer_rows)
            dst[mine, :] = src[mine, :]

        def end():
            lax.fori_loop(1, ents, wait, 0)

        return begin, end

    halo_begin, halo_end = exchange(halo_out, halo_in, halo_sems)
    back_begin, back_end = exchange(back_out, back_in, back_sems)
    halo_begin()

    build_group(y)
    adj_ref[all_slots] = jnp.zeros(adj_ref.shape[1:], BF16)
    for pair in rel_copies:
        pair[0].wait()
    meta = meta_ref[0]
    for k in range(1, groups):
        meta = meta + meta_ref[k]
    lanes = spots_vmem.shape[1]
    spots, coef, keys, by_row = arrange(meta, row_blocks, lanes)
    spots_vmem[...] = spots
    coef_vmem[...] = coef
    to_smem = [
        pltpu.make_async_copy(spots_vmem, spots_ref, load_sems.at[10]),
        pltpu.make_async_copy(coef_vmem, coef_ref, load_sems.at[11]),
    ]
    for copy in to_smem:
        copy.start()
    mate_copies = []
    for k in range(1, groups):
        group = lax.rem(y + k, groups)
        rel_copies[groups - 1 - k][1].wait()
        build_group(group)
        bases_copies[groups - 1 - k].wait()
        at = bases_ref.at[group * own_bases + core]
        copy = send(at, at, mate_sems, groups - k, mate, y)
        copy.start()
        mate_copies.append(copy)

    key = jnp.broadcast_to(meta[0:1] * row_blocks + meta[1:2], (all_slots, all_slots))
    live = jnp.broadcast_to(meta[3:4], (all_slots, all_slots))
    same = jnp.where(key == key.T, live, 0.0).astype(BF16)
    degree = jnp.dot(same, sums_ref[...].astype(BF16), preferred_element_type=F32)
    order = lax.broadcasted_iota(jnp.int32, (places, all_slots), 0).astype(F32)
    inv_ref[...] = jnp.dot(
        jnp.where(order == by_row, 1.0, 0.0),
        1.0 / jnp.maximum(degree, 1.0),
        preferred_element_type=F32,
        precision=HIGH,
    )
    for copy in to_smem:
        copy.wait()
    halo_end()
    for i in range(halo_rows // TILE):
        cols_ref[row_blocks + i] = halo_in[i * TILE : (i + 1) * TILE, :].astype(F32).T.astype(BF16)

    def spot(which, at, below):
        return jnp.minimum(jnp.maximum(spots_ref[which, at], 0), below - 1)

    def gather(n, carry):
        for i in range(STEP):
            p = n * STEP + i
            t = spot(0, p, all_slots + 1)
            value = jnp.dot(cols_ref[spot(2, t, cols_ref.shape[0])], adj_ref[t], preferred_element_type=F32)
            y_ref[p] = value * inv_ref[pl.ds(p, 1), :]
        return carry

    lax.fori_loop(0, steps, gather, 0)

    some = 32

    def mix(n, first):
        if not first:
            keep = spots_ref[1, n * STEP] == spots_ref[1, n * STEP - 1]
        for at in range(0, share, some):
            values = [y_ref[n * STEP + i, at : at + some, :] for i in range(STEP)]
            for b in range(bases_count):
                more = coef_ref[b, n * STEP] * values[0]
                for i in range(1, STEP):
                    more = more + coef_ref[b, n * STEP + i] * values[i]
                if not first:
                    before = runs_ref[(n - 1) * bases_count + b, at : at + some, :]
                    more = more + jnp.where(keep, before, 0.0)
                runs_ref[n * bases_count + b, at : at + some, :] = more

    mix(0, True)

    def mix_on(n, carry):
        mix(n, False)
        return carry

    lax.fori_loop(1, steps, mix_on, 0)
    loads[9].wait()
    each = own_bases
    strip = lines // each

    def outer(pair, carry):
        results = []
        for one in range(each):
            b = pair * each + one
            mixed = []
            for k in range(row_blocks):
                n = spot(8, k, steps) if k < row_blocks - 1 else steps - 1
                held = runs_ref[n * bases_count + b]
                mixed.append(jnp.where(spots_ref[9, k] > 0, held, 0.0))
            results.append(
                jnp.dot(
                    jnp.concatenate(mixed, axis=1).astype(BF16),
                    cot_ref[...],
                    preferred_element_type=F32,
                )
            )
        for z_at in range(zs):
            for core_at in range(cores):
                at = (z_at * cores + core_at) * strip
                basis_ref[core_at, pair, z_at] = jnp.concatenate(
                    [r[at : at + strip] for r in results], axis=0
                ).astype(BF16)
        return carry

    lax.fori_loop(0, bases_count // each, outer, 0)

    far = (2, 1, 3, 0)
    core_copies = {}
    for k in far:
        core_copies[k] = send(
            basis_ref.at[1 - core, lax.rem(x + k, xs)], core_in.at[k], core_sems, k, mate, y
        )
        core_copies[k].start()

    loads[8].wait()
    for copy in mate_copies:
        copy.wait()

    def prepare(b, carry):
        dm = lax.dot_general(
            bases_ref[b], cot_ref[...], (((1,), (1,)), ((), ())), preferred_element_type=F32
        )
        for k in range(row_blocks):
            dm_ref[k, b] = dm[:, k * TILE : (k + 1) * TILE].astype(BF16).astype(F32)
        return carry

    lax.fori_loop(0, bases_count, prepare, 0)

    x_copies = {}
    for k in far:
        core_copies[k].wait()
        to_x = lax.rem(x + k, xs)
        value = basis_ref[core, to_x].astype(F32) + core_in[k].astype(F32)
        if k == 0:
            x_sum[...] = value
        else:
            x_out[k] = value.astype(BF16)
            x_copies[k] = send(
                x_out.at[k], x_in.at[k], x_sems, k, ent(to_x, z, core), y
            )
            x_copies[k].start()

    rows = 16

    def pull(n, carry):
        k = spot(1, n * STEP, row_blocks)
        scale = [inv_ref[pl.ds(n * STEP + i, 1), :] for i in range(STEP)]
        coefs = [[coef_ref[b, n * STEP + i] for i in range(STEP)] for b in range(bases_count)]
        for at in range(0, share, rows):
            pulled = [None] * STEP
            for b in range(bases_count):
                dm = dm_ref[k, b, at : at + rows, :]
                for i in range(STEP):
                    term = coefs[b][i] * dm
                    pulled[i] = term if b == 0 else pulled[i] + term
            for i in range(STEP):
                z_ref[n * STEP + i, at : at + rows, :] = (pulled[i] * scale[i]).astype(BF16)
        return carry

    lax.fori_loop(0, steps, pull, 0)

    def scatter(q, carry):
        runs_ref[q] = lax.dot_general(
            adj_ref[spot(3, q, all_slots + 1)],
            z_ref[spot(4, q, places)],
            (((1,), (1,)), ((), ())),
            preferred_element_type=F32,
        )
        return carry

    half = all_slots // 2
    lax.fori_loop(0, half, scatter, 0, unroll=4)

    for k in range(1, xs):
        x_copies[k].wait()
    z_copies = []
    for k in range(1, zs):
        to_z = lax.rem(z + k, zs)
        value = x_sum[to_z]
        for j in range(1, xs):
            value = value + x_in[j, to_z].astype(F32)
        z_out[k] = value.astype(BF16)
        copy = send(z_out.at[k], z_in.at[k], z_sems, k, ent(x, to_z, core), y)
        copy.start()
        z_copies.append(copy)
    value = x_sum[z]
    for j in range(1, xs):
        value = value + x_in[j, z].astype(F32)

    lax.fori_loop(half, all_slots, scatter, 0, unroll=4)

    def run(q, held):
        held = runs_ref[q] + jnp.where(spots_ref[5, q] > 0, held, 0.0)
        runs_ref[q] = held
        return held

    lax.fori_loop(0, all_slots, run, jnp.zeros(runs_ref.shape[1:], F32), unroll=2)

    def column(c):
        return jnp.where(spots_ref[7, c] > 0, runs_ref[spot(6, c, all_slots)], 0.0)

    for i in range(halo_rows // TILE):
        back_out[i * TILE : (i + 1) * TILE, :] = column(row_blocks + i).astype(BF16)
    back_begin()

    def measure(n, carry):
        k = spot(1, n * STEP, row_blocks)
        inner = [[None] * bases_count for _ in range(STEP)]
        for at in range(0, share, rows):
            values = [y_ref[n * STEP + i, at : at + rows, :] for i in range(STEP)]
            for b in range(bases_count):
                dm = dm_ref[k, b, at : at + rows, :]
                for i in range(STEP):
                    term = values[i] * dm
                    term = term[:8] + term[8:]
                    inner[i][b] = term if at == 0 else inner[i][b] + term
        for i in range(STEP):
            for b in range(bases_count):
                inner_ref[b, pl.ds(n * STEP + i, 1), :] = jnp.sum(
                    inner[i][b], axis=0, keepdims=True
                )
        return carry

    lax.fori_loop(0, steps, measure, 0)

    parts_ref[...] = jnp.zeros_like(parts_ref)
    ones = jnp.ones((8, TILE), F32)
    for b in range(bases_count):
        summed = lax.dot_general(
            ones, inner_ref[b], (((1,), (1,)), ((), ())), preferred_element_type=F32, precision=HIGH
        )
        parts_ref[b : b + 1, :places] = summed[:1]
    c_rel_copies = [
        send(parts_ref, c_rel.at[k], c_rel_sems, k, d, lax.rem(y + k, groups))
        for k in range(1, groups)
    ]
    for copy in c_rel_copies:
        copy.start()

    for k in range(1, zs):
        z_copies[k - 1].wait()
        value = value + z_in[k].astype(F32)
    final_ref[...] = value.reshape(final_ref.shape)
    swap = send(final_ref, basis_out, swap_sems, 0, other, x)

    @pl.when(x != y)
    def _():
        swap.start()

    total = parts_ref[...]
    for k in range(1, groups):
        c_rel_copies[k - 1].wait()
        total = total + c_rel[k]
    padded = c_core.shape[2]
    relation = lax.broadcasted_iota(jnp.int32, (padded, lanes), 0) + y * rel_count
    hot = jnp.where(relation == keys, 1.0, 0.0)
    by_relation = lax.dot_general(
        total, hot, (((1,), (1,)), ((), ())), preferred_element_type=F32, precision=HIGH
    )
    c_core[0] = by_relation
    c_core_copy = send(c_core.at[0], c_core.at[1], c_core_sems, 0, mate, y)
    c_core_copy.start()

    for i in range(row_blocks):
        grads_out[i * TILE : (i + 1) * TILE, :] = column(i)
    step = 256
    for at in range(0, halo_rows, step):
        row = lax.broadcasted_iota(jnp.int32, (ent_rows, step), 0)
        hot_ref[:, at : at + step] = jnp.where(row == flat[:, at : at + step], 1.0, 0.0).astype(BF16)

    c_core_copy.wait()
    c_x[x] = c_core[0] + c_core[1]
    c_x_copies = [
        send(c_x.at[x], c_x.at[x], c_x_sems, k, ent(lax.rem(x + k, xs), z, core), y)
        for k in range(1, xs)
    ]
    for copy in c_x_copies:
        copy.start()

    for copy in c_x_copies:
        copy.wait()
    total = c_x[0]
    for j in range(1, xs):
        total = total + c_x[j]
    c_z[z] = total
    c_z_copies = [
        send(c_z.at[z], c_z.at[z], c_z_sems, k, ent(x, lax.rem(z + k, zs), core), y)
        for k in range(1, zs)
    ]
    for copy in c_z_copies:
        copy.start()

    back_end()
    grads_out[...] += jnp.dot(hot_ref[...], back_in[...], preferred_element_type=F32)

    for copy in c_z_copies:
        copy.wait()
    total = c_z[0]
    for j in range(1, zs):
        total = total + c_z[j]
    coeff_out[...] = total[:, :rel_count]

    @pl.when(x != y)
    def _():
        swap.wait()

    @pl.when(x == y)
    def _():
        basis_out[...] = final_ref[...]


def per_device(
    feats, cotangent, bases, coeffs, send_rows, tile_rel, tile_row, tile_col, tile_edges, tile_live
):
    ent_rows, width = feats.shape
    groups = lax.axis_size("rel")
    ents = lax.axis_size("ent")
    share = width // groups
    rel_count, bases_count = coeffs.shape
    slots = tile_rel.shape[1]
    all_slots = slots * groups
    row_blocks = ent_rows // TILE
    own_bases = bases.shape[0]
    halo_rows = send_rows.size
    col_blocks = (ent_rows + halo_rows) // TILE
    listed = tile_edges.shape[2]
    places = all_slots + row_blocks * STEP
    lanes = 2 * all_slots
    cores = 2
    zs = ents // (cores * groups)
    lines = own_bases * share // (cores * zs)
    padded = -(-rel_count // LANES) * LANES
    sems = pltpu.SemaphoreType.DMA
    shape = jax.ShapeDtypeStruct
    entity_grads, basis_grads, coeff_grads = pl.pallas_call(
        whole_kernel,
        out_shape=(
            shape((ent_rows, share), F32),
            shape((own_bases, lines // own_bases, width), F32),
            shape((bases_count, rel_count), F32),
        ),
        in_specs=[HBM] * 10,
        out_specs=(VMEM,) * 3,
        scratch_shapes=[
            pltpu.VMEM((ent_rows, share), BF16),
            pltpu.VMEM((ent_rows, width), BF16),
            pltpu.VMEM((bases_count, share, width), BF16),
            pltpu.VMEM((bases_count, rel_count), F32),
            pltpu.VMEM((send_rows.shape[1], ents), jnp.int32),
            pltpu.VMEM((1, slots), jnp.int32),
            pltpu.VMEM((1, slots), jnp.int32),
            pltpu.VMEM((1, slots), jnp.int32),
            pltpu.VMEM((1, 1), jnp.int32),
            pltpu.VMEM((all_slots, listed), jnp.int32),
            pltpu.VMEM((groups, 8 + bases_count, all_slots), F32),
            pltpu.VMEM((all_slots, TILE), F32),
            pltpu.VMEM((all_slots + 1, TILE, TILE), BF16),
            pltpu.VMEM((places, TILE), F32),
            pltpu.VMEM((col_blocks, share, TILE), BF16),
            pltpu.VMEM((16, lanes), jnp.int32),
            pltpu.VMEM((bases_count, lanes), F32),
            pltpu.SMEM((16, lanes), jnp.int32),
            pltpu.SMEM((bases_count, lanes), F32),
            pltpu.VMEM((places, share, TILE), F32),
            pltpu.VMEM((places // STEP * bases_count, share, TILE), F32),
            pltpu.VMEM((places, share, TILE), BF16),
            pltpu.VMEM((row_blocks, bases_count, share, TILE), F32),
            pltpu.VMEM((cores, groups, zs, lines, width), BF16),
            pltpu.VMEM((bases_count, places, TILE), F32),
            pltpu.VMEM((bases_count, lanes), F32),
            pltpu.VMEM((ent_rows, halo_rows), BF16),
            pltpu.VMEM((halo_rows, share), BF16),
            pltpu.VMEM((halo_rows, share), BF16),
            pltpu.VMEM((halo_rows, share), BF16),
            pltpu.VMEM((halo_rows, share), BF16),
            pltpu.VMEM((groups, zs, lines, width), BF16),
            pltpu.VMEM((groups, zs, lines, width), BF16),
            pltpu.VMEM((groups, zs, lines, width), BF16),
            pltpu.VMEM((zs, lines, width), F32),
            pltpu.VMEM((zs, lines, width), BF16),
            pltpu.VMEM((zs, lines, width), BF16),
            pltpu.VMEM((own_bases, lines // own_bases, width), F32),
            pltpu.VMEM((groups, bases_count, lanes), F32),
            pltpu.VMEM((2, bases_count, padded), F32),
            pltpu.VMEM((groups, bases_count, padded), F32),
            pltpu.VMEM((zs, bases_count, padded), F32),
            sems((12,)),
            sems((2, ents)),
            sems((2, groups)),
            sems((2, groups)),
            sems((2, groups)),
            sems((2, groups)),
            sems((2, ents)),
            sems((2, groups)),
            sems((2, groups)),
            sems((2, zs)),
            sems((2, 1)),
            sems((2, groups)),
            sems((2, 1)),
            sems((2, groups)),
            sems((2, zs)),
        ],
        compiler_params=pltpu.CompilerParams(
            collective_id=0, has_side_effects=True, vmem_limit_bytes=60 << 20
        ),
    )(
        feats,
        cotangent,
        bases,
        coeffs.T,
        send_rows.T,
        tile_rel,
        tile_row,
        tile_col,
        tile_edges,
        tile_live,
    )
    return entity_grads, basis_grads, coeff_grads.T


def solution(mesh):
    placed = (
        P("ent", None),
        P("ent", None),
        P("rel", None, None),
        P("rel", None),
        P("ent", None),
        P("ent", "rel"),
        P("ent", "rel"),
        P("ent", "rel"),
        P("ent", "rel", None),
        P("ent", "rel"),
    )
    return jax.shard_map(
        per_device,
        mesh=mesh,
        in_specs=placed,
        out_specs=(P("ent", "rel"), P("rel", "ent", None), P("rel", None)),
        check_vma=False,
    )
```

```python
import jax
import jax.numpy as jnp
from jax import lax
from jax.experimental import pallas as pl
from jax.experimental.pallas import tpu as pltpu
from jax.sharding import PartitionSpec as P

TILE = 128
LANES = 128
BF16 = jnp.bfloat16
F32 = jnp.float32
HIGH = lax.Precision.HIGHEST
VMEM = pl.BlockSpec(memory_space=pltpu.VMEM)
HBM = pl.BlockSpec(memory_space=pltpu.HBM)
STEP = 4
PAIR = 2


def lanes_to(value, count):
    return jnp.broadcast_to(value, (count, value.shape[1]))


def arrange(meta, row_blocks, places, empty):
    tiles = meta.shape[1]
    key, row, col, live = meta[0:1], meta[1:2], meta[2:3], meta[3:4]
    earlier = lax.broadcasted_iota(jnp.int32, (tiles, tiles), 0) < lax.broadcasted_iota(
        jnp.int32, (tiles, tiles), 1
    )
    at = lax.broadcasted_iota(jnp.int32, (1, places), 1).astype(F32)
    spot = lax.broadcasted_iota(jnp.int32, (tiles, places), 1).astype(F32)
    name = lax.broadcasted_iota(jnp.int32, (tiles, places), 0).astype(F32)

    def down(value):
        turned = lanes_to(value, tiles).T
        return jnp.concatenate([turned] * (places // tiles), axis=1)

    rows, cols = lanes_to(row, tiles), lanes_to(col, tiles)
    rows_d, cols_d, live_d = down(row), down(col), down(live)

    def count(mask):
        return jnp.sum(jnp.where(mask, live_d[:, :tiles], 0.0), axis=0, keepdims=True)

    before_row = count((rows_d[:, :tiles] == rows) & earlier)
    before_col = count((cols_d[:, :tiles] == cols) & earlier)
    start = jnp.zeros((1, 1), F32)
    by_row, block = before_row, jnp.zeros_like(at)
    last, filled = jnp.zeros_like(at), jnp.zeros_like(at)
    for k in range(row_blocks):
        held = jnp.sum(jnp.where(row == k, live, 0.0), axis=1, keepdims=True)
        filled = filled + jnp.where(at == k, jnp.where(held > 0, 1.0, 0.0), 0.0)
        start = start + jnp.floor((held + (STEP - 1)) * (1.0 / STEP)) * STEP
        if k < row_blocks - 1:
            last = last + jnp.where(at == k, jnp.maximum(start * (1.0 / STEP) - 1.0, 0.0), 0.0)
            block = block + jnp.where(at >= start, 1.0, 0.0)
            by_row = by_row + jnp.where(row > k, jnp.where(row == k + 1, start, 0.0), 0.0)
    by_row = jnp.where(live > 0, by_row, -1.0)
    own = jnp.sum(jnp.where(cols_d == spot, live_d, 0.0), axis=0, keepdims=True)
    padded = jnp.floor((own + (PAIR - 1)) * (1.0 / PAIR)) * PAIR
    padded_d = down(padded[:, :tiles])
    lower = jnp.where(name[:, :tiles] < cols, padded_d[:, :tiles], 0.0)
    by_col = jnp.where(live > 0, jnp.sum(lower, axis=0, keepdims=True) + before_col, -1.0)
    row_hot = jnp.where(down(by_row) == spot, 1.0, 0.0)
    col_hot = jnp.where(down(by_col) == spot, 1.0, 0.0)

    def pick(hot, value, empty):
        return jnp.sum(hot * (value - empty), axis=0, keepdims=True) + empty

    upto = jnp.sum(jnp.where(name <= spot, padded_d, 0.0), axis=0, keepdims=True)
    spots = [
        pick(row_hot, down(by_col), empty),
        block,
        pick(col_hot, cols_d, 0.0),
        pick(col_hot, name, float(tiles)),
        pick(col_hot, down(by_row), 0.0),
        pick(col_hot, down(jnp.where(before_col > 0, 1.0, 0.0)), 0.0),
        jnp.maximum(upto * (1.0 / PAIR) - 1.0, 0.0),
        jnp.where(own > 0, 1.0, 0.0),
        last,
        filled,
        jnp.zeros((6, places), F32),
    ]
    coef = jnp.dot(meta[8:16], row_hot, preferred_element_type=F32, precision=HIGH)
    keys = pick(row_hot, down(key), -1.0)
    return jnp.concatenate(spots, axis=0).astype(jnp.int32), coef, keys.astype(jnp.int32), by_row, by_col


def whole_kernel(
    feats_hbm,
    cot_hbm,
    bases_hbm,
    coeffs_hbm,
    send_hbm,
    rel_hbm,
    row_hbm,
    col_hbm,
    edges_hbm,
    live_hbm,
    grads_out,
    basis_out,
    coeff_out,
    feats_ref,
    cot_ref,
    bases_ref,
    coeffs_ref,
    send_ref,
    rel_ref,
    row_ref,
    col_ref,
    live_ref,
    lists_ref,
    meta_ref,
    sums_ref,
    adj_ref,
    inv_ref,
    col_inv_ref,
    cols_ref,
    spots_vmem,
    coef_vmem,
    spots_ref,
    coef_ref,
    y_ref,
    runs_ref,
    z_ref,
    dm_ref,
    basis_ref,
    inner_ref,
    parts_ref,
    hot_ref,
    halo_out,
    halo_in,
    back_out,
    back_in,
    core_in,
    x_out,
    x_in,
    x_sum,
    z_out,
    z_in,
    final_ref,
    c_rel,
    c_core,
    c_x,
    c_z,
    load_sems,
    halo_sems,
    bases_sems,
    mate_sems,
    lists_sems,
    meta_sems,
    back_sems,
    core_sems,
    x_sems,
    z_sems,
    swap_sems,
    c_rel_sems,
    c_core_sems,
    c_x_sems,
    c_z_sems,
):
    cores, xs, zs, lines, width = basis_ref.shape
    groups = xs
    ents = cores * xs * zs
    d, y = lax.axis_index("ent"), lax.axis_index("rel")
    core = lax.rem(d, cores)
    z = lax.rem(lax.div(d, cores), zs)
    x = lax.div(d, cores * zs)
    mate = d + 1 - 2 * core
    all_slots, listed = lists_ref.shape
    slots = all_slots // groups
    peer_rows = send_ref.shape[0]
    ent_rows, share = feats_ref.shape
    row_blocks = ent_rows // TILE
    bases_count, rel_count = coeffs_ref.shape
    own_bases = bases_count // groups
    halo_rows = ents * peer_rows
    places = inv_ref.shape[0]
    steps = places // STEP
    own_at = pl.ds(pl.multiple_of(y * share, share), share)
    own_slots = pl.ds(pl.multiple_of(y * slots, slots), slots)

    loads = [
        pltpu.make_async_copy(src, dst, load_sems.at[i])
        for i, (src, dst) in enumerate(
            (
                (rel_hbm, rel_ref),
                (row_hbm, row_ref),
                (col_hbm, col_ref),
                (live_hbm, live_ref),
                (coeffs_hbm, coeffs_ref),
                (edges_hbm.at[0], lists_ref.at[own_slots, :]),
                (send_hbm, send_ref),
                (feats_hbm.at[:, own_at], feats_ref),
                (bases_hbm.at[:, own_at, :], bases_ref.at[pl.ds(y * own_bases, own_bases)]),
                (cot_hbm, cot_ref),
            )
        )
    ]
    for load in loads:
        load.start()

    def ent(x_at, z_at, core_at):
        return (x_at * zs + z_at) * cores + core_at

    def send(src, dst, sems, at, to_ent, to_rel):
        return pltpu.make_async_remote_copy(
            src_ref=src,
            dst_ref=dst,
            send_sem=sems.at[0, at],
            recv_sem=sems.at[1, at],
            device_id=(to_ent, to_rel),
            device_id_type=pl.DeviceIdType.MESH,
        )

    barrier = pltpu.get_barrier_semaphore()

    def greet(to_ent, to_rel):
        pl.semaphore_signal(
            barrier, inc=1, device_id=(to_ent, to_rel), device_id_type=pl.DeviceIdType.MESH
        )

    for k in range(1, groups):
        greet(d, lax.rem(y + k, groups))
    other = ent(y, z, core)

    @pl.when(x != y)
    def _():
        greet(other, x)

    def greet_ent(off, carry):
        greet(lax.rem(d + off, ents), y)
        return carry

    lax.fori_loop(1, ents, greet_ent, 0)

    lane = lax.broadcasted_iota(jnp.int32, (slots, all_slots), 1)
    slot = lax.broadcasted_iota(jnp.int32, (slots, all_slots), 0)
    spread = jnp.where(lane == slot + y * slots, 1.0, 0.0)
    for load in loads[:7]:
        load.wait()
    order = lax.broadcasted_iota(jnp.int32, (1, slots), 1)
    alive = jnp.where(order < live_ref[...], 1.0, 0.0)
    rel = rel_ref[...]
    marks = jnp.concatenate(
        [
            (rel + y * rel_count).astype(F32),
            row_ref[...].astype(F32),
            col_ref[...].astype(F32),
            alive,
            jnp.zeros((4, slots), F32),
        ],
        axis=0,
    )
    rel_hot = jnp.where(
        lax.broadcasted_iota(jnp.int32, (rel_count, slots), 0) == rel, 1.0, 0.0
    )
    coef = jnp.dot(coeffs_ref[...], rel_hot, preferred_element_type=F32, precision=HIGH)
    meta_ref[y] = jnp.dot(
        jnp.concatenate([marks, coef], axis=0), spread, preferred_element_type=F32, precision=HIGH
    )

    place = lax.broadcasted_iota(jnp.int32, (TILE, listed), 0).astype(BF16)

    def build_group(group):
        def build(i, carry):
            t = group * slots + i
            edge = lists_ref[pl.ds(t, 1), :]
            to_col = (edge & (TILE - 1)).astype(BF16)
            to_row = (edge >> 7).astype(BF16)
            one, zero = jnp.ones((), BF16), jnp.zeros((), BF16)
            col_hot = jnp.where(place == to_col, one, zero)
            row_hot = jnp.where(place == to_row, one, zero)
            counts = lax.dot_general(
                col_hot, row_hot, (((1,), (1,)), ((), ())), preferred_element_type=F32
            )
            adj_ref[t] = counts.astype(BF16)
            sums_ref[pl.ds(t, 1), :] = jnp.sum(counts, axis=0, keepdims=True)
            return carry

        lax.fori_loop(0, slots, build, 0, unroll=8)

    pl.semaphore_wait(barrier, ents - 1 + groups - 1 + jnp.where(x != y, 1, 0))

    rel_copies, bases_copies = [], []
    for k in range(1, groups):
        to = lax.rem(y + k, groups)
        rel_copies.append(
            (
                send(meta_ref.at[y], meta_ref.at[y], meta_sems, k, d, to),
                send(lists_ref.at[own_slots, :], lists_ref.at[own_slots, :], lists_sems, k, d, to),
            )
        )
        bases_copies.append(
            send(
                bases_hbm.at[core, pl.ds(pl.multiple_of(to * share, share), share), :],
                bases_ref.at[y * own_bases + core],
                bases_sems,
                k,
                d,
                to,
            )
        )
    for pair in rel_copies:
        for copy in pair:
            copy.start()
    for copy in bases_copies:
        copy.start()

    def exchange(src, dst, sems):
        def of(off):
            to = lax.rem(d + off, ents)
            return send(
                src.at[pl.ds(pl.multiple_of(to * peer_rows, peer_rows), peer_rows), :],
                dst.at[pl.ds(pl.multiple_of(d * peer_rows, peer_rows), peer_rows), :],
                sems,
                off,
                to,
                y,
            )

        def start(off, carry):
            of(off).start()
            return carry

        def wait(off, carry):
            of(off).wait()
            return carry

        def begin():
            lax.fori_loop(1, ents, start, 0)
            mine = pl.ds(pl.multiple_of(d * peer_rows, peer_rows), peer_rows)
            dst[mine, :] = src[mine, :]

        def end():
            lax.fori_loop(1, ents, wait, 0)

        return begin, end

    halo_begin, halo_end = exchange(halo_out, halo_in, halo_sems)
    back_begin, back_end = exchange(back_out, back_in, back_sems)
    spot = lax.broadcasted_iota(jnp.int32, (ents, halo_rows), 1)
    peer = lax.broadcasted_iota(jnp.int32, (ents, halo_rows), 0)
    fan = jnp.where(lax.div(spot, peer_rows) == peer, 1.0, 0.0)
    fanned = jnp.dot(
        send_ref[...].astype(F32), fan, preferred_element_type=F32, precision=HIGH
    )
    spot = lax.broadcasted_iota(jnp.int32, (peer_rows, halo_rows), 1)
    inside = lax.broadcasted_iota(jnp.int32, (peer_rows, halo_rows), 0)
    flat = jnp.sum(
        jnp.where(lax.rem(spot, peer_rows) == inside, fanned, 0.0), axis=0, keepdims=True
    ).astype(jnp.int32)
    loads[7].wait()
    own = feats_ref[...].astype(F32)
    blocks = [own[i * TILE : (i + 1) * TILE, :].T.astype(BF16) for i in range(ent_rows // TILE)]
    for i, one in enumerate(blocks):
        cols_ref[i] = one
    own_t = jnp.concatenate(blocks, axis=1)
    row = lax.broadcasted_iota(jnp.int32, (ent_rows, TILE), 0)
    for i in range(halo_rows // TILE):
        hot = jnp.where(row == flat[:, i * TILE : (i + 1) * TILE], 1.0, 0.0).astype(BF16)
        picked = jnp.dot(own_t, hot, preferred_element_type=F32)
        halo_out[i * TILE : (i + 1) * TILE, :] = picked.T.astype(BF16)


    halo_begin()

    build_group(y)
    adj_ref[all_slots] = jnp.zeros(adj_ref.shape[1:], BF16)
    for pair in rel_copies:
        pair[0].wait()
    meta = meta_ref[0]
    for k in range(1, groups):
        meta = meta + meta_ref[k]
    lanes = spots_vmem.shape[1]
    spots, coef, keys, by_row, by_col = arrange(meta, row_blocks, lanes, float(places))
    spots_vmem[...] = spots
    coef_vmem[...] = coef
    to_smem = [
        pltpu.make_async_copy(spots_vmem, spots_ref, load_sems.at[10]),
        pltpu.make_async_copy(coef_vmem, coef_ref, load_sems.at[11]),
    ]
    for copy in to_smem:
        copy.start()
    mate_copies = []
    for k in range(1, groups):
        group = lax.rem(y + k, groups)
        rel_copies[groups - 1 - k][1].wait()
        build_group(group)
        bases_copies[groups - 1 - k].wait()
        at = bases_ref.at[group * own_bases + core]
        copy = send(at, at, mate_sems, groups - k, mate, y)
        copy.start()
        mate_copies.append(copy)

    key = jnp.broadcast_to(meta[0:1] * row_blocks + meta[1:2], (all_slots, all_slots))
    live = jnp.broadcast_to(meta[3:4], (all_slots, all_slots))
    same = jnp.where(key == key.T, live, 0.0).astype(BF16)
    degree = jnp.dot(same, sums_ref[...].astype(BF16), preferred_element_type=F32)
    order = lax.broadcasted_iota(jnp.int32, (places, all_slots), 0).astype(F32)
    inverse = 1.0 / jnp.maximum(degree, 1.0)
    for ref, by in ((inv_ref, by_row), (col_inv_ref, by_col)):
        ref[...] = jnp.dot(
            jnp.where(order == by, 1.0, 0.0), inverse, preferred_element_type=F32, precision=HIGH
        )
    for copy in to_smem:
        copy.wait()
    halo_end()
    for i in range(halo_rows // TILE):
        cols_ref[row_blocks + i] = halo_in[i * TILE : (i + 1) * TILE, :].astype(F32).T.astype(BF16)

    def spot(which, at, below):
        return jnp.minimum(jnp.maximum(spots_ref[which, at], 0), below - 1)

    def tiles_of(n):
        return jnp.concatenate(
            [adj_ref[spot(3, n * PAIR + i, all_slots + 1)] for i in range(PAIR)], axis=1
        )

    def gather(n, carry):
        at = n * PAIR
        columns = cols_ref[spot(2, at, cols_ref.shape[0])]
        value = jnp.dot(columns, tiles_of(n), preferred_element_type=F32)
        for i in range(PAIR):
            y_ref[at + i] = value[:, i * TILE : (i + 1) * TILE] * col_inv_ref[pl.ds(at + i, 1), :]
        return carry

    lax.fori_loop(0, places // PAIR, gather, 0, unroll=8)
    y_ref[places] = jnp.zeros(y_ref.shape[1:], F32)

    some = 64

    def mix(n, first):
        where = [spot(0, n * STEP + i, places + 1) for i in range(STEP)]
        if not first:
            keep = spots_ref[1, n * STEP] == spots_ref[1, n * STEP - 1]
        for at in range(0, share, some):
            values = [y_ref[where[i], at : at + some, :] for i in range(STEP)]
            for b in range(bases_count):
                more = coef_ref[b, n * STEP] * values[0]
                for i in range(1, STEP):
                    more = more + coef_ref[b, n * STEP + i] * values[i]
                if not first:
                    before = runs_ref[(n - 1) * bases_count + b, at : at + some, :]
                    more = more + jnp.where(keep, before, 0.0)
                runs_ref[n * bases_count + b, at : at + some, :] = more

    mix(0, True)

    def mix_on(n, carry):
        mix(n, False)
        return carry

    lax.fori_loop(1, steps, mix_on, 0)
    loads[9].wait()
    each = own_bases
    strip = lines // each

    def outer(pair, carry):
        results = []
        for one in range(each):
            b = pair * each + one
            mixed = []
            for k in range(row_blocks):
                n = spot(8, k, steps) if k < row_blocks - 1 else steps - 1
                held = runs_ref[n * bases_count + b]
                mixed.append(jnp.where(spots_ref[9, k] > 0, held, 0.0))
            results.append(
                jnp.dot(
                    jnp.concatenate(mixed, axis=1).astype(BF16),
                    cot_ref[...],
                    preferred_element_type=F32,
                )
            )
        for z_at in range(zs):
            for core_at in range(cores):
                at = (z_at * cores + core_at) * strip
                basis_ref[core_at, pair, z_at] = jnp.concatenate(
                    [r[at : at + strip] for r in results], axis=0
                ).astype(BF16)
        return carry

    lax.fori_loop(0, bases_count // each, outer, 0)

    far = (2, 1, 3, 0)
    core_copies = {}
    for k in far:
        core_copies[k] = send(
            basis_ref.at[1 - core, lax.rem(x + k, xs)], core_in.at[k], core_sems, k, mate, y
        )
        core_copies[k].start()

    loads[8].wait()
    for copy in mate_copies:
        copy.wait()

    def prepare(b, carry):
        dm = lax.dot_general(
            bases_ref[b], cot_ref[...], (((1,), (1,)), ((), ())), preferred_element_type=F32
        )
        for k in range(row_blocks):
            dm_ref[k, b] = dm[:, k * TILE : (k + 1) * TILE].astype(BF16).astype(F32)
        return carry

    lax.fori_loop(0, bases_count, prepare, 0)

    x_copies = {}
    for k in far:
        core_copies[k].wait()
        to_x = lax.rem(x + k, xs)
        value = basis_ref[core, to_x].astype(F32) + core_in[k].astype(F32)
        if k == 0:
            x_sum[...] = value
        else:
            x_out[k] = value.astype(BF16)
            x_copies[k] = send(
                x_out.at[k], x_in.at[k], x_sems, k, ent(to_x, z, core), y
            )
            x_copies[k].start()

    rows = 16
    def measure(n, carry):
        k = spot(1, n * STEP, row_blocks)
        where = [spot(0, n * STEP + i, places + 1) for i in range(STEP)]
        inner = [[None] * bases_count for _ in range(STEP)]
        for at in range(0, share, rows):
            values = [y_ref[where[i], at : at + rows, :] for i in range(STEP)]
            for b in range(bases_count):
                dm = dm_ref[k, b, at : at + rows, :]
                for i in range(STEP):
                    term = values[i] * dm
                    term = term[:8] + term[8:]
                    inner[i][b] = term if at == 0 else inner[i][b] + term
        for i in range(STEP):
            for b in range(bases_count):
                inner_ref[b, pl.ds(n * STEP + i, 1), :] = jnp.sum(
                    inner[i][b], axis=0, keepdims=True
                )
        return carry

    early = steps // 3
    lax.fori_loop(0, early, measure, 0, unroll=2)


    def pull(n, carry):
        k = spot(1, n * STEP, row_blocks)
        scale = [inv_ref[pl.ds(n * STEP + i, 1), :] for i in range(STEP)]
        coefs = [[coef_ref[b, n * STEP + i] for i in range(STEP)] for b in range(bases_count)]
        for at in range(0, share, rows):
            pulled = [None] * STEP
            for b in range(bases_count):
                dm = dm_ref[k, b, at : at + rows, :]
                for i in range(STEP):
                    term = coefs[b][i] * dm
                    pulled[i] = term if b == 0 else pulled[i] + term
            for i in range(STEP):
                z_ref[n * STEP + i, at : at + rows, :] = (pulled[i] * scale[i]).astype(BF16)
        return carry

    lax.fori_loop(0, steps, pull, 0, unroll=2)

    def scatter(n, carry):
        pulled = [z_ref[spot(4, n * PAIR + i, places)] for i in range(PAIR)]
        runs_ref[n] = lax.dot_general(
            tiles_of(n),
            jnp.concatenate(pulled, axis=1),
            (((1,), (1,)), ((), ())),
            preferred_element_type=F32,
        )
        return carry

    sums = places // PAIR
    half = sums // 2
    lax.fori_loop(0, half, scatter, 0, unroll=6)

    for k in range(1, xs):
        x_copies[k].wait()
    z_copies = []
    for k in range(1, zs):
        to_z = lax.rem(z + k, zs)
        value = x_sum[to_z]
        for j in range(1, xs):
            value = value + x_in[j, to_z].astype(F32)
        z_out[k] = value.astype(BF16)
        copy = send(z_out.at[k], z_in.at[k], z_sems, k, ent(x, to_z, core), y)
        copy.start()
        z_copies.append(copy)
    value = x_sum[z]
    for j in range(1, xs):
        value = value + x_in[j, z].astype(F32)

    lax.fori_loop(half, sums, scatter, 0, unroll=6)

    def run(q, held):
        held = runs_ref[q] + jnp.where(spots_ref[5, q * PAIR] > 0, held, 0.0)
        runs_ref[q] = held
        return held

    lax.fori_loop(0, sums, run, jnp.zeros(runs_ref.shape[1:], F32), unroll=4)

    def column(c):
        return jnp.where(spots_ref[7, c] > 0, runs_ref[spot(6, c, sums)], 0.0)

    for i in range(halo_rows // TILE):
        back_out[i * TILE : (i + 1) * TILE, :] = column(row_blocks + i).astype(BF16)
    back_begin()

    lax.fori_loop(early, steps, measure, 0, unroll=2)

    parts_ref[...] = jnp.zeros_like(parts_ref)
    ones = jnp.ones((8, TILE), F32)
    for b in range(bases_count):
        summed = lax.dot_general(
            ones, inner_ref[b], (((1,), (1,)), ((), ())), preferred_element_type=F32, precision=HIGH
        )
        parts_ref[b : b + 1, :places] = summed[:1]
    c_rel_copies = [
        send(parts_ref, c_rel.at[k], c_rel_sems, k, d, lax.rem(y + k, groups))
        for k in range(1, groups)
    ]
    for copy in c_rel_copies:
        copy.start()

    for k in range(1, zs):
        z_copies[k - 1].wait()
        value = value + z_in[k].astype(F32)
    final_ref[...] = value.reshape(final_ref.shape)
    swap = send(final_ref, basis_out, swap_sems, 0, other, x)

    @pl.when(x != y)
    def _():
        swap.start()

    total = parts_ref[...]
    for k in range(1, groups):
        c_rel_copies[k - 1].wait()
        total = total + c_rel[k]
    padded = c_core.shape[2]
    relation = lax.broadcasted_iota(jnp.int32, (padded, lanes), 0) + y * rel_count
    hot = jnp.where(relation == keys, 1.0, 0.0)
    by_relation = lax.dot_general(
        total, hot, (((1,), (1,)), ((), ())), preferred_element_type=F32, precision=HIGH
    )
    c_core[0] = by_relation
    c_core_copy = send(c_core.at[0], c_core.at[1], c_core_sems, 0, mate, y)
    c_core_copy.start()

    for i in range(row_blocks):
        grads_out[i * TILE : (i + 1) * TILE, :] = column(i)
    step = 256
    for at in range(0, halo_rows, step):
        row = lax.broadcasted_iota(jnp.int32, (ent_rows, step), 0)
        hot_ref[:, at : at + step] = jnp.where(row == flat[:, at : at + step], 1.0, 0.0).astype(BF16)

    c_core_copy.wait()
    c_x[x] = c_core[0] + c_core[1]
    c_x_copies = [
        send(c_x.at[x], c_x.at[x], c_x_sems, k, ent(lax.rem(x + k, xs), z, core), y)
        for k in range(1, xs)
    ]
    for copy in c_x_copies:
        copy.start()

    for copy in c_x_copies:
        copy.wait()
    total = c_x[0]
    for j in range(1, xs):
        total = total + c_x[j]
    c_z[z] = total
    c_z_copies = [
        send(c_z.at[z], c_z.at[z], c_z_sems, k, ent(x, lax.rem(z + k, zs), core), y)
        for k in range(1, zs)
    ]
    for copy in c_z_copies:
        copy.start()

    back_end()
    grads_out[...] += jnp.dot(hot_ref[...], back_in[...], preferred_element_type=F32)

    for copy in c_z_copies:
        copy.wait()
    total = c_z[0]
    for j in range(1, zs):
        total = total + c_z[j]
    coeff_out[...] = total[:, :rel_count]

    @pl.when(x != y)
    def _():
        swap.wait()

    @pl.when(x == y)
    def _():
        basis_out[...] = final_ref[...]


def per_device(
    feats, cotangent, bases, coeffs, send_rows, tile_rel, tile_row, tile_col, tile_edges, tile_live
):
    ent_rows, width = feats.shape
    groups = lax.axis_size("rel")
    ents = lax.axis_size("ent")
    share = width // groups
    rel_count, bases_count = coeffs.shape
    slots = tile_rel.shape[1]
    all_slots = slots * groups
    row_blocks = ent_rows // TILE
    own_bases = bases.shape[0]
    halo_rows = send_rows.size
    col_blocks = (ent_rows + halo_rows) // TILE
    listed = tile_edges.shape[2]
    places = all_slots + row_blocks * STEP
    lanes = 2 * all_slots
    cores = 2
    zs = ents // (cores * groups)
    lines = own_bases * share // (cores * zs)
    padded = -(-rel_count // LANES) * LANES
    sems = pltpu.SemaphoreType.DMA
    shape = jax.ShapeDtypeStruct
    entity_grads, basis_grads, coeff_grads = pl.pallas_call(
        whole_kernel,
        out_shape=(
            shape((ent_rows, share), F32),
            shape((own_bases, lines // own_bases, width), F32),
            shape((bases_count, rel_count), F32),
        ),
        in_specs=[HBM] * 10,
        out_specs=(VMEM,) * 3,
        scratch_shapes=[
            pltpu.VMEM((ent_rows, share), BF16),
            pltpu.VMEM((ent_rows, width), BF16),
            pltpu.VMEM((bases_count, share, width), BF16),
            pltpu.VMEM((bases_count, rel_count), F32),
            pltpu.VMEM((send_rows.shape[1], ents), jnp.int32),
            pltpu.VMEM((1, slots), jnp.int32),
            pltpu.VMEM((1, slots), jnp.int32),
            pltpu.VMEM((1, slots), jnp.int32),
            pltpu.VMEM((1, 1), jnp.int32),
            pltpu.VMEM((all_slots, listed), jnp.int32),
            pltpu.VMEM((groups, 8 + bases_count, all_slots), F32),
            pltpu.VMEM((all_slots, TILE), F32),
            pltpu.VMEM((all_slots + 1, TILE, TILE), BF16),
            pltpu.VMEM((places, TILE), F32),
            pltpu.VMEM((places, TILE), F32),
            pltpu.VMEM((col_blocks, share, TILE), BF16),
            pltpu.VMEM((16, lanes), jnp.int32),
            pltpu.VMEM((bases_count, lanes), F32),
            pltpu.SMEM((16, lanes), jnp.int32),
            pltpu.SMEM((bases_count, lanes), F32),
            pltpu.VMEM((places + 1, share, TILE), F32),
            pltpu.VMEM((places // STEP * bases_count, share, TILE), F32),
            pltpu.VMEM((places, share, TILE), BF16),
            pltpu.VMEM((row_blocks, bases_count, share, TILE), F32),
            pltpu.VMEM((cores, groups, zs, lines, width), BF16),
            pltpu.VMEM((bases_count, places, TILE), F32),
            pltpu.VMEM((bases_count, lanes), F32),
            pltpu.VMEM((ent_rows, halo_rows), BF16),
            pltpu.VMEM((halo_rows, share), BF16),
            pltpu.VMEM((halo_rows, share), BF16),
            pltpu.VMEM((halo_rows, share), BF16),
            pltpu.VMEM((halo_rows, share), BF16),
            pltpu.VMEM((groups, zs, lines, width), BF16),
            pltpu.VMEM((groups, zs, lines, width), BF16),
            pltpu.VMEM((groups, zs, lines, width), BF16),
            pltpu.VMEM((zs, lines, width), F32),
            pltpu.VMEM((zs, lines, width), BF16),
            pltpu.VMEM((zs, lines, width), BF16),
            pltpu.VMEM((own_bases, lines // own_bases, width), F32),
            pltpu.VMEM((groups, bases_count, lanes), F32),
            pltpu.VMEM((2, bases_count, padded), F32),
            pltpu.VMEM((groups, bases_count, padded), F32),
            pltpu.VMEM((zs, bases_count, padded), F32),
            sems((12,)),
            sems((2, ents)),
            sems((2, groups)),
            sems((2, groups)),
            sems((2, groups)),
            sems((2, groups)),
            sems((2, ents)),
            sems((2, groups)),
            sems((2, groups)),
            sems((2, zs)),
            sems((2, 1)),
            sems((2, groups)),
            sems((2, 1)),
            sems((2, groups)),
            sems((2, zs)),
        ],
        compiler_params=pltpu.CompilerParams(
            collective_id=0, has_side_effects=True, vmem_limit_bytes=60 << 20
        ),
    )(
        feats,
        cotangent,
        bases,
        coeffs.T,
        send_rows.T,
        tile_rel,
        tile_row,
        tile_col,
        tile_edges,
        tile_live,
    )
    return entity_grads, basis_grads, coeff_grads.T


def solution(mesh):
    placed = (
        P("ent", None),
        P("ent", None),
        P("rel", None, None),
        P("rel", None),
        P("ent", None),
        P("ent", "rel"),
        P("ent", "rel"),
        P("ent", "rel"),
        P("ent", "rel", None),
        P("ent", "rel"),
    )
    return jax.shard_map(
        per_device,
        mesh=mesh,
        in_specs=placed,
        out_specs=(P("ent", "rel"), P("rel", "ent", None), P("rel", None)),
        check_vma=False,
    )
```

```python
import jax
import jax.numpy as jnp
from jax import lax
from jax.experimental import pallas as pl
from jax.experimental.pallas import tpu as pltpu
from jax.sharding import PartitionSpec as P

TILE = 128
LANES = 128
BF16 = jnp.bfloat16
F32 = jnp.float32
HIGH = lax.Precision.HIGHEST
VMEM = pl.BlockSpec(memory_space=pltpu.VMEM)
HBM = pl.BlockSpec(memory_space=pltpu.HBM)
STEP = 4
PAIR = 2


def split(value):
    high = value.astype(BF16).astype(F32)
    rest = value - high
    middle = rest.astype(BF16).astype(F32)
    return high, middle, rest - middle


def by_hot(value, hot, axis):
    parts = jnp.concatenate(split(value), axis=0).astype(BF16)
    found = lax.dot_general(
        parts, hot.astype(BF16), (((1,), (axis,)), ((), ())), preferred_element_type=F32
    )
    n = value.shape[0]
    return found[:n] + (found[n : 2 * n] + found[2 * n :])


def lanes_to(value, count):
    return jnp.broadcast_to(value, (count, value.shape[1]))


def arrange(meta, row_blocks, places, empty):
    tiles = meta.shape[1]
    key, row, col, live = meta[0:1], meta[1:2], meta[2:3], meta[3:4]
    earlier = lax.broadcasted_iota(jnp.int32, (tiles, tiles), 0) < lax.broadcasted_iota(
        jnp.int32, (tiles, tiles), 1
    )
    at = lax.broadcasted_iota(jnp.int32, (1, places), 1).astype(F32)
    spot = lax.broadcasted_iota(jnp.int32, (tiles, places), 1).astype(F32)
    name = lax.broadcasted_iota(jnp.int32, (tiles, places), 0).astype(F32)

    def down(value):
        turned = lanes_to(value, tiles).T
        return jnp.concatenate([turned] * (places // tiles), axis=1)

    rows, cols = lanes_to(row, tiles), lanes_to(col, tiles)
    rows_d, cols_d, live_d = down(row), down(col), down(live)

    def count(mask):
        return jnp.sum(jnp.where(mask, live_d[:, :tiles], 0.0), axis=0, keepdims=True)

    before_row = count((rows_d[:, :tiles] == rows) & earlier)
    before_col = count((cols_d[:, :tiles] == cols) & earlier)
    start = jnp.zeros((1, 1), F32)
    by_row, block = before_row, jnp.zeros_like(at)
    last, filled = jnp.zeros_like(at), jnp.zeros_like(at)
    for k in range(row_blocks):
        held = jnp.sum(jnp.where(row == k, live, 0.0), axis=1, keepdims=True)
        filled = filled + jnp.where(at == k, jnp.where(held > 0, 1.0, 0.0), 0.0)
        start = start + jnp.floor((held + (STEP - 1)) * (1.0 / STEP)) * STEP
        if k < row_blocks - 1:
            last = last + jnp.where(at == k, jnp.maximum(start * (1.0 / STEP) - 1.0, 0.0), 0.0)
            block = block + jnp.where(at >= start, 1.0, 0.0)
            by_row = by_row + jnp.where(row > k, jnp.where(row == k + 1, start, 0.0), 0.0)
    by_row = jnp.where(live > 0, by_row, -1.0)
    own = jnp.sum(jnp.where(cols_d == spot, live_d, 0.0), axis=0, keepdims=True)
    padded = jnp.floor((own + (PAIR - 1)) * (1.0 / PAIR)) * PAIR
    padded_d = down(padded[:, :tiles])
    lower = jnp.where(name[:, :tiles] < cols, padded_d[:, :tiles], 0.0)
    by_col = jnp.where(live > 0, jnp.sum(lower, axis=0, keepdims=True) + before_col, -1.0)
    row_hot = jnp.where(down(by_row) == spot, 1.0, 0.0)
    col_hot = jnp.where(down(by_col) == spot, 1.0, 0.0)

    def pick(hot, value, empty):
        return jnp.sum(hot * (value - empty), axis=0, keepdims=True) + empty

    upto = jnp.sum(jnp.where(name <= spot, padded_d, 0.0), axis=0, keepdims=True)
    spots = [
        pick(row_hot, down(by_col), empty),
        block,
        pick(col_hot, cols_d, 0.0),
        pick(col_hot, name, float(tiles)),
        pick(col_hot, down(by_row), 0.0),
        pick(col_hot, down(jnp.where(before_col > 0, 1.0, 0.0)), 0.0),
        jnp.maximum(upto * (1.0 / PAIR) - 1.0, 0.0),
        jnp.where(own > 0, 1.0, 0.0),
        last,
        filled,
        jnp.zeros((6, places), F32),
    ]
    coef = by_hot(meta[8:16], row_hot, 0)
    keys = pick(row_hot, down(key), -1.0)
    return jnp.concatenate(spots, axis=0).astype(jnp.int32), coef, keys.astype(jnp.int32), by_row, by_col


def whole_kernel(
    feats_hbm,
    cot_hbm,
    bases_hbm,
    coeffs_hbm,
    send_hbm,
    rel_hbm,
    row_hbm,
    col_hbm,
    edges_hbm,
    live_hbm,
    grads_out,
    basis_out,
    coeff_out,
    feats_ref,
    cot_ref,
    bases_ref,
    coeffs_ref,
    send_ref,
    rel_ref,
    row_ref,
    col_ref,
    live_ref,
    lists_ref,
    meta_ref,
    sums_ref,
    adj_ref,
    inv_ref,
    col_inv_ref,
    cols_ref,
    spots_vmem,
    coef_vmem,
    spots_ref,
    coef_ref,
    y_ref,
    runs_ref,
    z_ref,
    dm_ref,
    basis_ref,
    inner_ref,
    parts_ref,
    hot_ref,
    halo_out,
    halo_in,
    back_out,
    back_in,
    core_in,
    x_out,
    x_in,
    x_sum,
    z_out,
    z_in,
    final_ref,
    c_rel,
    c_core,
    c_x,
    c_z,
    load_sems,
    halo_sems,
    bases_sems,
    mate_sems,
    lists_sems,
    meta_sems,
    back_sems,
    core_sems,
    x_sems,
    z_sems,
    swap_sems,
    c_rel_sems,
    c_core_sems,
    c_x_sems,
    c_z_sems,
):
    cores, xs, zs, lines, width = basis_ref.shape
    groups = xs
    ents = cores * xs * zs
    d, y = lax.axis_index("ent"), lax.axis_index("rel")
    core = lax.rem(d, cores)
    z = lax.rem(lax.div(d, cores), zs)
    x = lax.div(d, cores * zs)
    mate = d + 1 - 2 * core
    all_slots, listed = lists_ref.shape
    slots = all_slots // groups
    peer_rows = send_ref.shape[0]
    ent_rows, share = feats_ref.shape
    row_blocks = ent_rows // TILE
    bases_count, rel_count = coeffs_ref.shape
    own_bases = bases_count // groups
    halo_rows = ents * peer_rows
    places = inv_ref.shape[0]
    steps = places // STEP
    own_at = pl.ds(pl.multiple_of(y * share, share), share)
    own_slots = pl.ds(pl.multiple_of(y * slots, slots), slots)

    loads = [
        pltpu.make_async_copy(src, dst, load_sems.at[i])
        for i, (src, dst) in enumerate(
            (
                (rel_hbm, rel_ref),
                (row_hbm, row_ref),
                (col_hbm, col_ref),
                (live_hbm, live_ref),
                (coeffs_hbm, coeffs_ref),
                (edges_hbm.at[0], lists_ref.at[own_slots, :]),
                (send_hbm, send_ref),
                (feats_hbm.at[:, own_at], feats_ref),
                (bases_hbm.at[:, own_at, :], bases_ref.at[pl.ds(y * own_bases, own_bases)]),
                (cot_hbm, cot_ref),
            )
        )
    ]
    for load in loads:
        load.start()

    def ent(x_at, z_at, core_at):
        return (x_at * zs + z_at) * cores + core_at

    def send(src, dst, sems, at, to_ent, to_rel):
        return pltpu.make_async_remote_copy(
            src_ref=src,
            dst_ref=dst,
            send_sem=sems.at[0, at],
            recv_sem=sems.at[1, at],
            device_id=(to_ent, to_rel),
            device_id_type=pl.DeviceIdType.MESH,
        )

    barrier = pltpu.get_barrier_semaphore()

    def greet(to_ent, to_rel):
        pl.semaphore_signal(
            barrier, inc=1, device_id=(to_ent, to_rel), device_id_type=pl.DeviceIdType.MESH
        )

    for k in range(1, groups):
        greet(d, lax.rem(y + k, groups))
    other = ent(y, z, core)

    @pl.when(x != y)
    def _():
        greet(other, x)

    def greet_ent(off, carry):
        greet(lax.rem(d + off, ents), y)
        return carry

    lax.fori_loop(1, ents, greet_ent, 0)

    lane = lax.broadcasted_iota(jnp.int32, (slots, all_slots), 1)
    slot = lax.broadcasted_iota(jnp.int32, (slots, all_slots), 0)
    spread = jnp.where(lane == slot + y * slots, 1.0, 0.0)
    for load in loads[:7]:
        load.wait()
    order = lax.broadcasted_iota(jnp.int32, (1, slots), 1)
    alive = jnp.where(order < live_ref[...], 1.0, 0.0)
    rel = rel_ref[...]
    marks = jnp.concatenate(
        [
            (rel + y * rel_count).astype(F32),
            row_ref[...].astype(F32),
            col_ref[...].astype(F32),
            alive,
            jnp.zeros((4, slots), F32),
        ],
        axis=0,
    )
    rel_hot = jnp.where(
        lax.broadcasted_iota(jnp.int32, (rel_count, slots), 0) == rel, 1.0, 0.0
    )
    coef = jnp.dot(coeffs_ref[...], rel_hot, preferred_element_type=F32, precision=HIGH)
    meta_ref[y] = jnp.dot(
        jnp.concatenate([marks, coef], axis=0), spread, preferred_element_type=F32, precision=HIGH
    )

    place = lax.broadcasted_iota(jnp.int32, (TILE, listed), 0).astype(BF16)

    def build_group(group):
        def build(i, carry):
            t = group * slots + i
            edge = lists_ref[pl.ds(t, 1), :]
            to_col = (edge & (TILE - 1)).astype(BF16)
            to_row = (edge >> 7).astype(BF16)
            one, zero = jnp.ones((), BF16), jnp.zeros((), BF16)
            col_hot = jnp.where(place == to_col, one, zero)
            row_hot = jnp.where(place == to_row, one, zero)
            counts = lax.dot_general(
                col_hot, row_hot, (((1,), (1,)), ((), ())), preferred_element_type=F32
            )
            adj_ref[t] = counts.astype(BF16)
            sums_ref[pl.ds(t, 1), :] = jnp.sum(counts, axis=0, keepdims=True)
            return carry

        lax.fori_loop(0, slots, build, 0, unroll=8)

    pl.semaphore_wait(barrier, ents - 1 + groups - 1 + jnp.where(x != y, 1, 0))

    rel_copies, bases_copies = [], []
    for k in range(1, groups):
        to = lax.rem(y + k, groups)
        rel_copies.append(
            (
                send(meta_ref.at[y], meta_ref.at[y], meta_sems, k, d, to),
                send(lists_ref.at[own_slots, :], lists_ref.at[own_slots, :], lists_sems, k, d, to),
            )
        )
        bases_copies.append(
            send(
                bases_hbm.at[core, pl.ds(pl.multiple_of(to * share, share), share), :],
                bases_ref.at[y * own_bases + core],
                bases_sems,
                k,
                d,
                to,
            )
        )
    for pair in rel_copies:
        for copy in pair:
            copy.start()
    for copy in bases_copies:
        copy.start()

    def exchange(src, dst, sems):
        def of(off):
            to = lax.rem(d + off, ents)
            return send(
                src.at[pl.ds(pl.multiple_of(to * peer_rows, peer_rows), peer_rows), :],
                dst.at[pl.ds(pl.multiple_of(d * peer_rows, peer_rows), peer_rows), :],
                sems,
                off,
                to,
                y,
            )

        def start(off, carry):
            of(off).start()
            return carry

        def wait(off, carry):
            of(off).wait()
            return carry

        def begin():
            lax.fori_loop(1, ents, start, 0)
            mine = pl.ds(pl.multiple_of(d * peer_rows, peer_rows), peer_rows)
            dst[mine, :] = src[mine, :]

        def end():
            lax.fori_loop(1, ents, wait, 0)

        return begin, end

    halo_begin, halo_end = exchange(halo_out, halo_in, halo_sems)
    back_begin, back_end = exchange(back_out, back_in, back_sems)
    spot = lax.broadcasted_iota(jnp.int32, (ents, halo_rows), 1)
    peer = lax.broadcasted_iota(jnp.int32, (ents, halo_rows), 0)
    fan = jnp.where(lax.div(spot, peer_rows) == peer, 1.0, 0.0)
    fanned = by_hot(send_ref[...].astype(F32), fan, 0)
    spot = lax.broadcasted_iota(jnp.int32, (peer_rows, halo_rows), 1)
    inside = lax.broadcasted_iota(jnp.int32, (peer_rows, halo_rows), 0)
    flat = jnp.sum(
        jnp.where(lax.rem(spot, peer_rows) == inside, fanned, 0.0), axis=0, keepdims=True
    ).astype(jnp.int32)
    loads[7].wait()
    own = feats_ref[...].astype(F32)
    blocks = [own[i * TILE : (i + 1) * TILE, :].T.astype(BF16) for i in range(ent_rows // TILE)]
    for i, one in enumerate(blocks):
        cols_ref[i] = one
    own_t = jnp.concatenate(blocks, axis=1)
    row = lax.broadcasted_iota(jnp.int32, (ent_rows, TILE), 0)
    for i in range(halo_rows // TILE):
        hot = jnp.where(row == flat[:, i * TILE : (i + 1) * TILE], 1.0, 0.0).astype(BF16)
        picked = jnp.dot(own_t, hot, preferred_element_type=F32)
        halo_out[i * TILE : (i + 1) * TILE, :] = picked.T.astype(BF16)


    halo_begin()

    build_group(y)
    adj_ref[all_slots] = jnp.zeros(adj_ref.shape[1:], BF16)
    for pair in rel_copies:
        pair[0].wait()
    meta = meta_ref[0]
    for k in range(1, groups):
        meta = meta + meta_ref[k]
    lanes = spots_vmem.shape[1]
    spots, coef, keys, by_row, by_col = arrange(meta, row_blocks, lanes, float(places))
    spots_vmem[...] = spots
    coef_vmem[...] = coef
    to_smem = [
        pltpu.make_async_copy(spots_vmem, spots_ref, load_sems.at[10]),
        pltpu.make_async_copy(coef_vmem, coef_ref, load_sems.at[11]),
    ]
    for copy in to_smem:
        copy.start()
    mate_copies = []
    for k in range(1, groups):
        group = lax.rem(y + k, groups)
        rel_copies[groups - 1 - k][1].wait()
        build_group(group)
        bases_copies[groups - 1 - k].wait()
        at = bases_ref.at[group * own_bases + core]
        copy = send(at, at, mate_sems, groups - k, mate, y)
        copy.start()
        mate_copies.append(copy)

    key = jnp.broadcast_to(meta[0:1] * row_blocks + meta[1:2], (all_slots, all_slots))
    live = jnp.broadcast_to(meta[3:4], (all_slots, all_slots))
    same = jnp.where(key == key.T, live, 0.0).astype(BF16)
    degree = jnp.dot(same, sums_ref[...].astype(BF16), preferred_element_type=F32)
    order = lax.broadcasted_iota(jnp.int32, (places, all_slots), 0).astype(F32)
    inverse = 1.0 / jnp.maximum(degree, 1.0)
    for ref, by in ((inv_ref, by_row), (col_inv_ref, by_col)):
        ref[...] = jnp.dot(
            jnp.where(order == by, 1.0, 0.0), inverse, preferred_element_type=F32, precision=HIGH
        )
    for copy in to_smem:
        copy.wait()
    halo_end()
    for i in range(halo_rows // TILE):
        cols_ref[row_blocks + i] = halo_in[i * TILE : (i + 1) * TILE, :].astype(F32).T.astype(BF16)

    def spot(which, at, below):
        return jnp.minimum(jnp.maximum(spots_ref[which, at], 0), below - 1)

    def tiles_of(n):
        return jnp.concatenate(
            [adj_ref[spot(3, n * PAIR + i, all_slots + 1)] for i in range(PAIR)], axis=1
        )

    def gather(n, carry):
        at = n * PAIR
        columns = cols_ref[spot(2, at, cols_ref.shape[0])]
        value = jnp.dot(columns, tiles_of(n), preferred_element_type=F32)
        for i in range(PAIR):
            y_ref[at + i] = value[:, i * TILE : (i + 1) * TILE] * col_inv_ref[pl.ds(at + i, 1), :]
        return carry

    lax.fori_loop(0, places // PAIR, gather, 0, unroll=8)
    y_ref[places] = jnp.zeros(y_ref.shape[1:], F32)

    some = 64

    def mix(n, first):
        where = [spot(0, n * STEP + i, places + 1) for i in range(STEP)]
        if not first:
            keep = spots_ref[1, n * STEP] == spots_ref[1, n * STEP - 1]
        for at in range(0, share, some):
            values = [y_ref[where[i], at : at + some, :] for i in range(STEP)]
            for b in range(bases_count):
                more = coef_ref[b, n * STEP] * values[0]
                for i in range(1, STEP):
                    more = more + coef_ref[b, n * STEP + i] * values[i]
                if not first:
                    before = runs_ref[(n - 1) * bases_count + b, at : at + some, :]
                    more = more + jnp.where(keep, before, 0.0)
                runs_ref[n * bases_count + b, at : at + some, :] = more

    mix(0, True)

    def mix_on(n, carry):
        mix(n, False)
        return carry

    lax.fori_loop(1, steps, mix_on, 0, unroll=5)
    loads[9].wait()
    each = own_bases
    strip = lines // each

    def outer(pair, carry):
        results = []
        for one in range(each):
            b = pair * each + one
            mixed = []
            for k in range(row_blocks):
                n = spot(8, k, steps) if k < row_blocks - 1 else steps - 1
                held = runs_ref[n * bases_count + b]
                mixed.append(jnp.where(spots_ref[9, k] > 0, held, 0.0))
            results.append(
                jnp.dot(
                    jnp.concatenate(mixed, axis=1).astype(BF16),
                    cot_ref[...],
                    preferred_element_type=F32,
                )
            )
        for z_at in range(zs):
            for core_at in range(cores):
                at = (z_at * cores + core_at) * strip
                basis_ref[core_at, pair, z_at] = jnp.concatenate(
                    [r[at : at + strip] for r in results], axis=0
                ).astype(BF16)
        return carry

    lax.fori_loop(0, bases_count // each, outer, 0)

    far = (2, 1, 3, 0)
    core_copies = {}
    for k in far:
        core_copies[k] = send(
            basis_ref.at[1 - core, lax.rem(x + k, xs)], core_in.at[k], core_sems, k, mate, y
        )
        core_copies[k].start()

    loads[8].wait()
    for copy in mate_copies:
        copy.wait()

    def prepare(b, carry):
        dm = lax.dot_general(
            bases_ref[b], cot_ref[...], (((1,), (1,)), ((), ())), preferred_element_type=F32
        )
        for k in range(row_blocks):
            dm_ref[k, b] = dm[:, k * TILE : (k + 1) * TILE].astype(BF16).astype(F32)
        return carry

    lax.fori_loop(0, bases_count, prepare, 0)

    x_copies = {}
    for k in far:
        core_copies[k].wait()
        to_x = lax.rem(x + k, xs)
        value = basis_ref[core, to_x].astype(F32) + core_in[k].astype(F32)
        if k == 0:
            x_sum[...] = value
        else:
            x_out[k] = value.astype(BF16)
            x_copies[k] = send(
                x_out.at[k], x_in.at[k], x_sems, k, ent(to_x, z, core), y
            )
            x_copies[k].start()

    rows = 16
    def measure(n, carry):
        k = spot(1, n * STEP, row_blocks)
        where = [spot(0, n * STEP + i, places + 1) for i in range(STEP)]
        inner = [[None] * bases_count for _ in range(STEP)]
        for at in range(0, share, rows):
            values = [y_ref[where[i], at : at + rows, :] for i in range(STEP)]
            for b in range(bases_count):
                dm = dm_ref[k, b, at : at + rows, :]
                for i in range(STEP):
                    term = values[i] * dm
                    term = term[:8] + term[8:]
                    inner[i][b] = term if at == 0 else inner[i][b] + term
        for i in range(STEP):
            for b in range(bases_count):
                inner_ref[b, pl.ds(n * STEP + i, 1), :] = jnp.sum(
                    inner[i][b], axis=0, keepdims=True
                )
        return carry

    early = steps // 3
    lax.fori_loop(0, early, measure, 0, unroll=2)


    def pull(n, carry):
        k = spot(1, n * STEP, row_blocks)
        scale = [inv_ref[pl.ds(n * STEP + i, 1), :] for i in range(STEP)]
        coefs = [[coef_ref[b, n * STEP + i] for i in range(STEP)] for b in range(bases_count)]
        for at in range(0, share, rows):
            pulled = [None] * STEP
            for b in range(bases_count):
                dm = dm_ref[k, b, at : at + rows, :]
                for i in range(STEP):
                    term = coefs[b][i] * dm
                    pulled[i] = term if b == 0 else pulled[i] + term
            for i in range(STEP):
                z_ref[n * STEP + i, at : at + rows, :] = (pulled[i] * scale[i]).astype(BF16)
        return carry

    lax.fori_loop(0, steps, pull, 0, unroll=2)

    def scatter(n, carry):
        pulled = [z_ref[spot(4, n * PAIR + i, places)] for i in range(PAIR)]
        runs_ref[n] = lax.dot_general(
            tiles_of(n),
            jnp.concatenate(pulled, axis=1),
            (((1,), (1,)), ((), ())),
            preferred_element_type=F32,
        )
        return carry

    sums = places // PAIR
    half = sums // 2
    lax.fori_loop(0, half, scatter, 0, unroll=6)

    for k in range(1, xs):
        x_copies[k].wait()
    z_copies = []
    for k in range(1, zs):
        to_z = lax.rem(z + k, zs)
        value = x_sum[to_z]
        for j in range(1, xs):
            value = value + x_in[j, to_z].astype(F32)
        z_out[k] = value.astype(BF16)
        copy = send(z_out.at[k], z_in.at[k], z_sems, k, ent(x, to_z, core), y)
        copy.start()
        z_copies.append(copy)
    value = x_sum[z]
    for j in range(1, xs):
        value = value + x_in[j, z].astype(F32)

    lax.fori_loop(half, sums, scatter, 0, unroll=6)

    def run(q, held):
        held = runs_ref[q] + jnp.where(spots_ref[5, q * PAIR] > 0, held, 0.0)
        runs_ref[q] = held
        return held

    lax.fori_loop(0, sums, run, jnp.zeros(runs_ref.shape[1:], F32), unroll=4)

    def column(c):
        return jnp.where(spots_ref[7, c] > 0, runs_ref[spot(6, c, sums)], 0.0)

    for i in range(halo_rows // TILE):
        back_out[i * TILE : (i + 1) * TILE, :] = column(row_blocks + i).astype(BF16)
    back_begin()

    lax.fori_loop(early, steps, measure, 0, unroll=2)

    parts_ref[...] = jnp.zeros_like(parts_ref)
    ones = jnp.ones((8, TILE), BF16)
    for b in range(bases_count):
        summed = sum(
            lax.dot_general(
                ones, part.astype(BF16), (((1,), (1,)), ((), ())), preferred_element_type=F32
            )
            for part in split(inner_ref[b])
        )
        parts_ref[b : b + 1, :places] = summed[:1]
    c_rel_copies = [
        send(parts_ref, c_rel.at[k], c_rel_sems, k, d, lax.rem(y + k, groups))
        for k in range(1, groups)
    ]
    for copy in c_rel_copies:
        copy.start()

    for k in range(1, zs):
        z_copies[k - 1].wait()
        value = value + z_in[k].astype(F32)
    final_ref[...] = value.reshape(final_ref.shape)
    swap = send(final_ref, basis_out, swap_sems, 0, other, x)

    @pl.when(x != y)
    def _():
        swap.start()

    total = parts_ref[...]
    for k in range(1, groups):
        c_rel_copies[k - 1].wait()
        total = total + c_rel[k]
    padded = c_core.shape[2]
    relation = lax.broadcasted_iota(jnp.int32, (padded, lanes), 0) + y * rel_count
    hot = jnp.where(relation == keys, 1.0, 0.0)
    by_relation = by_hot(total, hot, 1)
    c_core[0] = by_relation
    c_core_copy = send(c_core.at[0], c_core.at[1], c_core_sems, 0, mate, y)
    c_core_copy.start()

    for i in range(row_blocks):
        grads_out[i * TILE : (i + 1) * TILE, :] = column(i)
    step = 256
    for at in range(0, halo_rows, step):
        row = lax.broadcasted_iota(jnp.int32, (ent_rows, step), 0)
        hot_ref[:, at : at + step] = jnp.where(row == flat[:, at : at + step], 1.0, 0.0).astype(BF16)

    c_core_copy.wait()
    c_x[x] = c_core[0] + c_core[1]
    c_x_copies = [
        send(c_x.at[x], c_x.at[x], c_x_sems, k, ent(lax.rem(x + k, xs), z, core), y)
        for k in range(1, xs)
    ]
    for copy in c_x_copies:
        copy.start()

    for copy in c_x_copies:
        copy.wait()
    total = c_x[0]
    for j in range(1, xs):
        total = total + c_x[j]
    c_z[z] = total
    c_z_copies = [
        send(c_z.at[z], c_z.at[z], c_z_sems, k, ent(x, lax.rem(z + k, zs), core), y)
        for k in range(1, zs)
    ]
    for copy in c_z_copies:
        copy.start()

    back_end()
    grads_out[...] += jnp.dot(hot_ref[...], back_in[...], preferred_element_type=F32)

    for copy in c_z_copies:
        copy.wait()
    total = c_z[0]
    for j in range(1, zs):
        total = total + c_z[j]
    coeff_out[...] = total[:, :rel_count]

    @pl.when(x != y)
    def _():
        swap.wait()

    @pl.when(x == y)
    def _():
        basis_out[...] = final_ref[...]


def per_device(
    feats, cotangent, bases, coeffs, send_rows, tile_rel, tile_row, tile_col, tile_edges, tile_live
):
    ent_rows, width = feats.shape
    groups = lax.axis_size("rel")
    ents = lax.axis_size("ent")
    share = width // groups
    rel_count, bases_count = coeffs.shape
    slots = tile_rel.shape[1]
    all_slots = slots * groups
    row_blocks = ent_rows // TILE
    own_bases = bases.shape[0]
    halo_rows = send_rows.size
    col_blocks = (ent_rows + halo_rows) // TILE
    listed = tile_edges.shape[2]
    places = all_slots + row_blocks * STEP
    lanes = 2 * all_slots
    cores = 2
    zs = ents // (cores * groups)
    lines = own_bases * share // (cores * zs)
    padded = -(-rel_count // LANES) * LANES
    sems = pltpu.SemaphoreType.DMA
    shape = jax.ShapeDtypeStruct
    entity_grads, basis_grads, coeff_grads = pl.pallas_call(
        whole_kernel,
        out_shape=(
            shape((ent_rows, share), F32),
            shape((own_bases, lines // own_bases, width), F32),
            shape((bases_count, rel_count), F32),
        ),
        in_specs=[HBM] * 10,
        out_specs=(VMEM,) * 3,
        scratch_shapes=[
            pltpu.VMEM((ent_rows, share), BF16),
            pltpu.VMEM((ent_rows, width), BF16),
            pltpu.VMEM((bases_count, share, width), BF16),
            pltpu.VMEM((bases_count, rel_count), F32),
            pltpu.VMEM((send_rows.shape[1], ents), jnp.int32),
            pltpu.VMEM((1, slots), jnp.int32),
            pltpu.VMEM((1, slots), jnp.int32),
            pltpu.VMEM((1, slots), jnp.int32),
            pltpu.VMEM((1, 1), jnp.int32),
            pltpu.VMEM((all_slots, listed), jnp.int32),
            pltpu.VMEM((groups, 8 + bases_count, all_slots), F32),
            pltpu.VMEM((all_slots, TILE), F32),
            pltpu.VMEM((all_slots + 1, TILE, TILE), BF16),
            pltpu.VMEM((places, TILE), F32),
            pltpu.VMEM((places, TILE), F32),
            pltpu.VMEM((col_blocks, share, TILE), BF16),
            pltpu.VMEM((16, lanes), jnp.int32),
            pltpu.VMEM((bases_count, lanes), F32),
            pltpu.SMEM((16, lanes), jnp.int32),
            pltpu.SMEM((bases_count, lanes), F32),
            pltpu.VMEM((places + 1, share, TILE), F32),
            pltpu.VMEM((places // STEP * bases_count, share, TILE), F32),
            pltpu.VMEM((places, share, TILE), BF16),
            pltpu.VMEM((row_blocks, bases_count, share, TILE), F32),
            pltpu.VMEM((cores, groups, zs, lines, width), BF16),
            pltpu.VMEM((bases_count, places, TILE), F32),
            pltpu.VMEM((bases_count, lanes), F32),
            pltpu.VMEM((ent_rows, halo_rows), BF16),
            pltpu.VMEM((halo_rows, share), BF16),
            pltpu.VMEM((halo_rows, share), BF16),
            pltpu.VMEM((halo_rows, share), BF16),
            pltpu.VMEM((halo_rows, share), BF16),
            pltpu.VMEM((groups, zs, lines, width), BF16),
            pltpu.VMEM((groups, zs, lines, width), BF16),
            pltpu.VMEM((groups, zs, lines, width), BF16),
            pltpu.VMEM((zs, lines, width), F32),
            pltpu.VMEM((zs, lines, width), BF16),
            pltpu.VMEM((zs, lines, width), BF16),
            pltpu.VMEM((own_bases, lines // own_bases, width), F32),
            pltpu.VMEM((groups, bases_count, lanes), F32),
            pltpu.VMEM((2, bases_count, padded), F32),
            pltpu.VMEM((groups, bases_count, padded), F32),
            pltpu.VMEM((zs, bases_count, padded), F32),
            sems((12,)),
            sems((2, ents)),
            sems((2, groups)),
            sems((2, groups)),
            sems((2, groups)),
            sems((2, groups)),
            sems((2, ents)),
            sems((2, groups)),
            sems((2, groups)),
            sems((2, zs)),
            sems((2, 1)),
            sems((2, groups)),
            sems((2, 1)),
            sems((2, groups)),
            sems((2, zs)),
        ],
        compiler_params=pltpu.CompilerParams(
            collective_id=0, has_side_effects=True, vmem_limit_bytes=60 << 20
        ),
    )(
        feats,
        cotangent,
        bases,
        coeffs.T,
        send_rows.T,
        tile_rel,
        tile_row,
        tile_col,
        tile_edges,
        tile_live,
    )
    return entity_grads, basis_grads, coeff_grads.T


def solution(mesh):
    placed = (
        P("ent", None),
        P("ent", None),
        P("rel", None, None),
        P("rel", None),
        P("ent", None),
        P("ent", "rel"),
        P("ent", "rel"),
        P("ent", "rel"),
        P("ent", "rel", None),
        P("ent", "rel"),
    )
    return jax.shard_map(
        per_device,
        mesh=mesh,
        in_specs=placed,
        out_specs=(P("ent", "rel"), P("rel", "ent", None), P("rel", None)),
        check_vma=False,
    )
```
